32 devices in a mesh: groups: 2 (over y), member: 2 (over x), fsdp: 8 (over z, core).
Axes of the slice: x: 2, y: 2, z: 4, core: 2. Of those that a mesh axis runs over, the one named last changes fastest.
Arguments:
- gate_pre: bfloat16 [12288, 2560], P(('groups', 'member', 'fsdp')), parts along dimension 0, may hold values from -6 to 6
- up_pre: bfloat16 [12288, 2560], P(('groups', 'member', 'fsdp')), parts along dimension 0, may hold values from -6 to 6
- out_grad: bfloat16 [12288, 2048], P(('groups', 'member', 'fsdp')), parts along dimension 0, may hold values from -6 to 6
- in_scale: float32 [4, 2560], P('member'), may hold values from 0.1 to 1.9
- out_scale: float32 [4, 2048], P('member'), may hold values from 0.1 to 1.9
- down_weight: bfloat16 [2560, 2048], P('fsdp'), may hold values from -0.125 to 0.125
- member_slot: int32 [12288], P(('groups', 'member', 'fsdp')), parts along dimension 0, may hold values from 0 to 1, as said below
Outputs:
- grad_gate: bfloat16 [12288, 2560], P(('groups', 'member', 'fsdp')), parts along dimension 0
- grad_up: bfloat16 [12288, 2560], P(('groups', 'member', 'fsdp')), parts along dimension 0
- grad_down: float32 [5120, 2048], P(('groups', 'fsdp'), 'member'), parts along dimension 0
- grad_in_scale: float32 [8, 2560], P(('groups', 'member')), parts along dimension 0
- grad_out_scale: float32 [8, 2048], P(('groups', 'member')), parts along dimension 0
The draws below stay inside these ranges and needn't reach their ends.
There are 2 independent parts, one for each index of `groups`. The reference program is written for one: setup_inputs(seed, part) draws one part's arguments, and reference() takes and returns one part's arrays. A program takes and returns all parts, laid end to end along the dimension named above; an argument that names none is the same for every part. Nothing has to cross between parts.
Inputs may be any that keep to these rules, and one draw needn't show every extreme that they name: `member_slot`: constant over each sequence of 1024 tokens; the first sequence uses slot 1.
All inputs are finite; a program needn't handle non-finite values.
Results may differ from the reference program's by a relative error of at most 0.0051.
Values may be sent and summed in bfloat16 or wider, within the bound.
No kernel may reach another device: no remote copies, remote signals or barrier semaphores. Data moves between devices by JAX's collectives and lax.ppermute only.
A program may use at most 128 MiB of HBM per device.

```python
import jax
import jax.numpy as jnp
from jax import lax

D = 2048
FF = 2560
SEQ_LEN = 1024
MEM_DEV = 2
MEMBERS = 4
TOKENS = 6144


def draw_member_slot(key, part):
    key = jax.random.fold_in(key, 7)
    count = TOKENS // SEQ_LEN
    picks = jax.random.randint(key, (count,), 0, MEM_DEV, dtype=jnp.int32)
    picks = picks.at[0].set(MEM_DEV - 1)
    return jnp.repeat(picks, SEQ_LEN, total_repeat_length=TOKENS)


def block_scale(key, extent, split, low, top_value):
    factor_of = 1.0
    for axis_at, shards_of in split:
        heights = jax.random.uniform(jax.random.fold_in(jax.random.fold_in(key, 6), axis_at), (shards_of,), jnp.float32, low / len(split), top_value / len(split))
        factor_of = factor_of * jnp.repeat(jnp.exp(heights), extent[axis_at] // shards_of).reshape((-1,) + (1,) * (len(extent) - 1 - axis_at))
    return factor_of


def centred(own_key, extent, spread, reach, pieces=(), held_as=jnp.bfloat16):
    level = block_scale(own_key, extent, pieces, -0.22, 0.18) if pieces else 1.0
    result = jax.random.normal(own_key, extent, jnp.float32) * spread * level
    return jnp.minimum(jnp.maximum(result, -reach), reach).astype(held_as)


def setup_inputs(seed: int = 0, part: int = 0) -> dict:
    splits = jax.random.split(jax.random.key(seed), 8)
    part_splits = jax.random.split(jax.random.fold_in(splits[7], part), 8)
    gate_pre = centred(part_splits[0], (TOKENS, FF), 1.0, 6.0, ((0, 16),))
    up_pre = centred(part_splits[1], (TOKENS, FF), 1.0, 6.0, ((0, 16),))
    out_grad = centred(part_splits[2], (TOKENS, D), 1.0, 6.0, ((0, 16),))
    in_scale = jnp.clip(1.0 + 0.18 * jax.random.normal(splits[3], (MEMBERS, FF), jnp.float32), 0.1, 1.9)
    out_scale = jnp.clip(1.0 + 0.18 * jax.random.normal(splits[4], (MEMBERS, D), jnp.float32), 0.1, 1.9)
    down_weight = centred(splits[5], (FF, D), FF ** -0.5, 0.125, ((0, 8),))
    member_slot = draw_member_slot(jax.random.fold_in(jax.random.fold_in(splits[7], part), 71), part)
    return dict(gate_pre=gate_pre, up_pre=up_pre, out_grad=out_grad, in_scale=in_scale, out_scale=out_scale, down_weight=down_weight, member_slot=member_slot)


def gelu_tanh(value):
    return jax.nn.gelu(value, approximate=True)

def reference(gate_pre, up_pre, out_grad, in_scale, out_scale, down_weight, member_slot):
    block = TOKENS // MEMBERS * MEM_DEV
    positions = jnp.arange(TOKENS, dtype=jnp.int32)
    member_id = MEM_DEV * (positions // block) + member_slot
    onehot = (member_id[:, None] == jnp.arange(MEMBERS, dtype=jnp.int32)[None, :]).astype(jnp.float32)
    row_in = jnp.dot(onehot, in_scale, precision=lax.Precision.HIGHEST)
    row_out = jnp.dot(onehot, out_scale, precision=lax.Precision.HIGHEST)
    gate32 = gate_pre.astype(jnp.float32)
    up32 = up_pre.astype(jnp.float32)
    gelu_val, gelu_back = jax.vjp(gelu_tanh, gate32)
    act = gelu_val * up32
    hidden = (act * row_in).astype(jnp.bfloat16)
    grad32 = out_grad.astype(jnp.float32)
    scaled = (grad32 * row_out).astype(jnp.bfloat16)
    forward = jnp.dot(hidden, down_weight, preferred_element_type=jnp.float32)
    grad_out_scale = jnp.dot(onehot.T, grad32 * forward, precision=lax.Precision.HIGHEST)
    grad_hidden = jnp.dot(scaled, down_weight.T, preferred_element_type=jnp.float32)
    grad_in_scale = jnp.dot(onehot.T, grad_hidden * act, precision=lax.Precision.HIGHEST)
    grad_act = grad_hidden * row_in
    grad_gelu, = gelu_back(grad_act * up32)
    grad_gate = grad_gelu.astype(jnp.bfloat16)
    grad_up = (grad_act * gelu_val).astype(jnp.bfloat16)
    grad_down = jnp.dot(hidden.T, scaled, preferred_element_type=jnp.float32)
    return (grad_gate, grad_up, grad_down, grad_in_scale, grad_out_scale)
```

```python
import functools
import math

import jax
import jax.numpy as jnp
from jax import lax
from jax.experimental import pallas as pl
from jax.experimental.pallas import tpu as pltpu
from jax.sharding import PartitionSpec as P

F32 = jnp.float32
BF16 = jnp.bfloat16
VMEM_BYTES = 40 * 1024 * 1024
ROOT_2_PI = math.sqrt(2.0 / math.pi)
CUBIC = 0.044715


def tanh_of(x):
    return jnp.tanh(ROOT_2_PI * (x + CUBIC * (x * x * x)))


def pick_rows(slot, scale):
    rows = jnp.zeros((slot.shape[0], scale.shape[1]), F32)
    for k in range(scale.shape[0]):
        rows = jnp.where(slot == k, scale[k : k + 1, :], rows)
    return rows


def hidden_kernel(lo, core_ref, gate_ref, up_ref, in_scale_ref, slot_ref, *refs):
    outs, turned = refs[:lo], refs[lo]
    gate = gate_ref[...].astype(F32)
    gelu = gate * (0.5 * (1.0 + tanh_of(gate)))
    act = gelu * up_ref[...].astype(F32)
    hidden = act * pick_rows(slot_ref[...], in_scale_ref[...])
    turned[...] = hidden.T.astype(BF16)
    rows = turned.shape[0] // lo
    for j in range(lo):
        start = pl.multiple_of(lax.rem(core_ref[0] + j, lo) * rows, rows)
        outs[j][0] = turned[pl.ds(start, rows), :]


def hidden_turned(core, gate, up, in_scale, slot, blocks, lo):
    tokens, ff = gate.shape
    width = ff // blocks
    rows = width // lo
    column = pl.BlockSpec((tokens, width), lambda i, core: (0, i))
    return pl.pallas_call(
        functools.partial(hidden_kernel, lo),
        out_shape=[jax.ShapeDtypeStruct((blocks, rows, tokens), BF16)] * lo,
        grid_spec=pltpu.PrefetchScalarGridSpec(
            num_scalar_prefetch=1,
            grid=(blocks,),
            in_specs=[
                column,
                column,
                pl.BlockSpec((in_scale.shape[0], width), lambda i, core: (0, i)),
                pl.BlockSpec((tokens, 1), lambda i, core: (0, 0)),
            ],
            out_specs=[pl.BlockSpec((1, rows, tokens), lambda i, core: (i, 0, 0))] * lo,
            scratch_shapes=[pltpu.VMEM((width, tokens), BF16)],
        ),
        compiler_params=pltpu.CompilerParams(vmem_limit_bytes=VMEM_BYTES),
        cost_estimate=pl.CostEstimate(
            flops=20 * tokens * ff, bytes_accessed=6 * tokens * ff, transcendentals=tokens * ff
        ),
    )(core, gate, up, in_scale, slot)


def partial_kernel(lo, n_add, ids_ref, *refs):
    lefts, rights, adds, out_ref = refs[:lo], refs[lo : 2 * lo], refs[2 * lo : -1], refs[-1]
    total = adds[0][...].astype(F32) if n_add else None
    for i in range(1, n_add):
        total = total + adds[i][...].astype(F32)
    for left, right in zip(lefts, rights):
        term = jnp.dot(left[0], right[...], preferred_element_type=F32)
        total = term if total is None else total + term
    out_ref[...] = total.astype(out_ref.dtype)


def partial_block(block, column, lefts, rights, members, adds, dtype):
    lo = len(lefts)
    _, rows, tokens = lefts[0].shape
    width = rights[0].shape[1] // members
    ids = jnp.stack([block, column]).astype(jnp.int32)
    whole = pl.BlockSpec((rows, width), lambda i, ids: (0, 0))
    return pl.pallas_call(
        functools.partial(partial_kernel, lo, len(adds)),
        out_shape=jax.ShapeDtypeStruct((rows, width), dtype),
        grid_spec=pltpu.PrefetchScalarGridSpec(
            num_scalar_prefetch=1,
            grid=(1,),
            in_specs=[pl.BlockSpec((1, rows, tokens), lambda i, ids: (ids[0], 0, 0))] * lo
            + [pl.BlockSpec((tokens, width), lambda i, ids: (0, ids[1]))] * lo
            + [whole] * len(adds),
            out_specs=whole,
        ),
        compiler_params=pltpu.CompilerParams(vmem_limit_bytes=VMEM_BYTES),
        cost_estimate=pl.CostEstimate(
            flops=2 * lo * rows * tokens * width,
            bytes_accessed=2 * lo * tokens * (rows + width) + 4 * rows * width,
            transcendentals=0,
        ),
    )(ids, *lefts, *rights, *adds)


def slot_kernel(
    n_alias,
    ids_ref,
    weight_ref,
    scaled_ref,
    out_grad_ref,
    gate_ref,
    up_ref,
    in_scale_ref,
    slot_ref,
    *refs,
):
    grad_gate_ref, grad_up_ref, sum_in_ref, sum_out_ref = refs[n_alias:]
    weight = weight_ref[...]
    grad_hidden = lax.dot_general(
        scaled_ref[...], weight, (((1,), (1,)), ((), ())), preferred_element_type=F32
    )
    slot = slot_ref[...]
    gate = gate_ref[...].astype(F32)
    up = up_ref[...].astype(F32)
    tanh = tanh_of(gate)
    cdf = 0.5 * (1.0 + tanh)
    slope = cdf + gate * (0.5 * ROOT_2_PI) * (1.0 - tanh * tanh) * (
        1.0 + (3.0 * CUBIC) * (gate * gate)
    )
    gelu = gate * cdf
    act = gelu * up
    row_in = pick_rows(slot, in_scale_ref[...])
    hidden = (act * row_in).astype(BF16)
    grad_act = grad_hidden * row_in
    grad_gate_ref[...] = (grad_act * up * slope).astype(BF16)
    grad_up_ref[...] = (grad_act * gelu).astype(BF16)
    product = grad_hidden * act
    forward = jnp.dot(hidden, weight, preferred_element_type=F32)
    forward = forward * out_grad_ref[...].astype(F32)
    for k in range(in_scale_ref.shape[0]):
        mine = slot == k
        sum_in_ref[k : k + 1, :] = jnp.sum(jnp.where(mine, product, 0.0), axis=0, keepdims=True)
        sum_out_ref[k : k + 1, :] = jnp.sum(jnp.where(mine, forward, 0.0), axis=0, keepdims=True)


def weight_slot(block, weight, scaled, out_grad, gate, up, in_scale, slot, kept):
    tokens, ff = gate.shape
    width, d = weight.shape
    mem = in_scale.shape[0]
    ids = jnp.reshape(block, (1,)).astype(jnp.int32)
    column = pl.BlockSpec((tokens, width), lambda i, ids: (0, ids[0]))
    full = lambda shape: pl.BlockSpec(shape, lambda i, ids: (0, 0))
    ins = [weight, scaled, out_grad, gate, up, in_scale, slot]
    specs = [
        full((width, d)),
        full((tokens, d)),
        full((tokens, d)),
        column,
        column,
        pl.BlockSpec((mem, width), lambda i, ids: (0, ids[0])),
        full((tokens, 1)),
    ]
    aliases = {}
    if kept is not None:
        aliases = {1 + len(ins): 0, 2 + len(ins): 1}
        ins += list(kept)
        specs += [pl.BlockSpec(memory_space=pl.ANY)] * 2
    return pl.pallas_call(
        functools.partial(slot_kernel, len(aliases)),
        out_shape=[
            jax.ShapeDtypeStruct((tokens, ff), BF16),
            jax.ShapeDtypeStruct((tokens, ff), BF16),
            jax.ShapeDtypeStruct((mem, width), F32),
            jax.ShapeDtypeStruct((mem, d), F32),
        ],
        grid_spec=pltpu.PrefetchScalarGridSpec(
            num_scalar_prefetch=1,
            grid=(1,),
            in_specs=specs,
            out_specs=[column, column, full((mem, width)), full((mem, d))],
        ),
        input_output_aliases=aliases,
        compiler_params=pltpu.CompilerParams(vmem_limit_bytes=VMEM_BYTES),
        cost_estimate=pl.CostEstimate(
            flops=4 * tokens * width * d,
            bytes_accessed=2 * width * d + 4 * tokens * d + 8 * tokens * width,
            transcendentals=tokens * width,
        ),
    )(ids, *ins)


def place(pieces, me):
    n, rows = len(pieces), pieces[0].shape[0]
    if n == 1:
        return pieces[0]
    if n == 2:
        first = me == 0
        return jnp.concatenate(
            [jnp.where(first, pieces[0], pieces[1]), jnp.where(first, pieces[1], pieces[0])]
        )
    whole = jnp.zeros((n * rows,) + pieces[0].shape[1:], pieces[0].dtype)
    for j, piece in enumerate(pieces):
        whole = lax.dynamic_update_slice_in_dim(whole, piece, lax.rem(me + j, n) * rows, 0)
    return whole


def on_device(groups, members, fsdp):
    def run(gate, up, out_grad, in_scale, out_scale, weight, member_slot):
        tokens, ff = gate.shape
        shard = weight.shape[0]
        lo = 128 // math.gcd(shard, 128)
        line = fsdp // lo
        group = lax.axis_index("groups")
        member = lax.axis_index("member")
        place_id = lax.axis_index("fsdp")
        z, core = place_id // lo, lax.rem(place_id, lo)
        lower = z < line // 2
        slot = member_slot[:, None]

        def along_line(x, sources, step):
            pairs = [(s * lo + c, (s + step) * lo + c) for s in sources for c in range(lo)]
            return lax.ppermute(x, "fsdp", pairs)

        def within_chip(x, j):
            pairs = [
                (s * lo + (c + j) % lo, s * lo + c) for s in range(line) for c in range(lo)
            ]
            return lax.ppermute(x, "fsdp", pairs)

        def cyclic(x, axis, n, j):
            return lax.ppermute(x, axis, [((i + j) % n, i) for i in range(n)])

        part = shard // groups
        piece = lax.dynamic_slice_in_dim(weight, group * part, part, 0)
        ups, downs = [piece], [piece]
        for s in range(1, line):
            ups.append(along_line(ups[-1], range(s - 1, line - 1), 1))
            downs.append(along_line(downs[-1], range(1, line - s + 1), -1))

        scaled = (out_grad.astype(F32) * pick_rows(slot, out_scale)).astype(BF16)
        turned = hidden_turned(
            jnp.reshape(core, (1,)).astype(jnp.int32), gate, up, in_scale, slot, line, lo
        )
        lefts, rights = [turned[0]], [scaled]
        for j in range(1, lo):
            rights.append(within_chip(scaled, j))
            lefts.append(within_chip(turned[(lo - j) % lo], j))

        sums = [None] * line
        for k in list(range(1, line)) + [0]:
            block = lax.rem(jnp.where(lower, z - k, z + k) + line, line)
            got = []
            for j in range(1, members):
                to = lax.rem(member + members - j, members)
                send = partial_block(block, to, lefts, rights, members, [], BF16)
                got.append(cyclic(send, "member", members, j))
            sums[k] = partial_block(block, member, lefts, rights, members, got, F32)

        from_below = from_above = None
        for s in range(1, line):
            send_up = send_down = sums[s]
            if 2 * s > line:
                send_up = jnp.where(lower, sums[s], sums[line - s])
                send_down = jnp.where(lower, sums[line - s], sums[s])
            if from_below is not None:
                send_up = send_up + from_below.astype(F32)
                send_down = send_down + from_above.astype(F32)
            from_below = along_line(send_up.astype(BF16), range(s), 1)
            from_above = along_line(send_down.astype(BF16), range(line - s, line), -1)
        grad_down = sums[0] + from_below.astype(F32) + from_above.astype(F32)

        kept, sums_in, sum_out = None, jnp.zeros((in_scale.shape[0], ff), F32), None
        for j in range(line):
            block = lax.rem(jnp.where(lower, z + j, z - j) + line, line)
            if j == 0:
                rows = weight
            else:
                mine = jnp.where(lower, downs[j], ups[j])
                if 2 * j > line:
                    mine = jnp.where(
                        lower,
                        jnp.where(z + j < line, downs[j], ups[line - j]),
                        jnp.where(z >= j, ups[j], downs[line - j]),
                    )
                parts = [mine] + [cyclic(mine, "groups", groups, i) for i in range(1, groups)]
                rows = place(parts, group)
            rows = place([rows] + [within_chip(rows, i) for i in range(1, lo)], core)
            *kept, sum_in, more = weight_slot(
                block, rows, scaled, out_grad, gate, up, in_scale, slot, kept
            )
            sums_in = lax.dynamic_update_slice_in_dim(
                sums_in, sum_in, block * sum_in.shape[1], 1
            )
            sum_out = more if sum_out is None else sum_out + more
        both = jnp.concatenate([sums_in, sum_out], axis=1)
        if fsdp & (fsdp - 1):
            both = lax.psum(both, "fsdp")
        else:
            stage = 1
            while stage < fsdp:
                both = both + lax.ppermute(both, "fsdp", [(i, i ^ stage) for i in range(fsdp)])
                stage *= 2
        return kept[0], kept[1], grad_down, both[:, :ff], both[:, ff:]

    return run


def solution(mesh):
    rows = P(("groups", "member", "fsdp"), None)
    in_specs = (
        rows,
        rows,
        rows,
        P("member", None),
        P("member", None),
        P("fsdp", None),
        P(("groups", "member", "fsdp")),
    )
    out_specs = (
        rows,
        rows,
        P(("groups", "fsdp"), "member"),
        P(("groups", "member"), None),
        P(("groups", "member"), None),
    )
    run = on_device(mesh.shape["groups"], mesh.shape["member"], mesh.shape["fsdp"])
    return jax.shard_map(run, mesh=mesh, in_specs=in_specs, out_specs=out_specs, check_vma=False)
```

```python
import functools
import math

import jax
import jax.numpy as jnp
from jax import lax
from jax.experimental import pallas as pl
from jax.experimental.pallas import tpu as pltpu
from jax.sharding import PartitionSpec as P

F32 = jnp.float32
BF16 = jnp.bfloat16
VMEM_BYTES = 60 * 1024 * 1024
ROOT_2_PI = math.sqrt(2.0 / math.pi)
CUBIC = 0.044715
SHORT = pl.CostEstimate(flops=1, bytes_accessed=1, transcendentals=0)


def tanh_of(x):
    return jnp.tanh(ROOT_2_PI * (x + CUBIC * (x * x * x)))


def pick_rows(slot, scale):
    rows = jnp.zeros((slot.shape[0], scale.shape[1]), F32)
    for k in range(scale.shape[0]):
        rows = jnp.where(slot == k, scale[k : k + 1, :], rows)
    return rows


def prepare_kernel(nh, gate_ref, up_ref, in_scale_ref, grad_ref, out_scale_ref, slot_ref, *outs):
    slot = slot_ref[...]
    gate = gate_ref[...].astype(F32)
    gelu = gate * (0.5 * (1.0 + tanh_of(gate)))
    act = gelu * up_ref[...].astype(F32)
    turned = (act * pick_rows(slot, in_scale_ref[...])).T.astype(BF16)
    shard = outs[0].shape[1] // nh
    for i in range(nh):
        for p in range(2):
            first = (2 * i + p) * shard
            outs[p][0, i * shard : (i + 1) * shard, :] = turned[first : first + shard]
    scaled = (grad_ref[...].astype(F32) * pick_rows(slot, out_scale_ref[...])).astype(BF16)
    half = scaled.shape[0] // 2
    outs[2][...] = scaled[:half]
    outs[3][...] = scaled[half:]


def prepare(gate, up, in_scale, out_grad, out_scale, slot, blocks, nh):
    tokens, ff = gate.shape
    d = out_grad.shape[1]
    width, columns = ff // blocks, d // blocks
    mem = in_scale.shape[0]
    spec = lambda shape: pl.BlockSpec(shape, lambda i: (0, i))
    turned = jax.ShapeDtypeStruct((blocks, width // 2, tokens), BF16)
    scaled = jax.ShapeDtypeStruct((tokens // 2, d), BF16)
    return pl.pallas_call(
        functools.partial(prepare_kernel, nh),
        out_shape=[turned, turned, scaled, scaled],
        grid=(blocks,),
        in_specs=[
            spec((tokens, width)),
            spec((tokens, width)),
            spec((mem, width)),
            spec((tokens, columns)),
            spec((mem, columns)),
            pl.BlockSpec((tokens, 1), lambda i: (0, 0)),
        ],
        out_specs=[pl.BlockSpec((1, width // 2, tokens), lambda i: (i, 0, 0))] * 2
        + [spec((tokens // 2, columns))] * 2,
        compiler_params=pltpu.CompilerParams(vmem_limit_bytes=VMEM_BYTES),
        cost_estimate=SHORT,
    )(gate, up, in_scale, out_grad, out_scale, slot)


def partials_kernel(lo, items, n_columns, own_at, ids_ref, *refs):
    lefts, refs = [refs[2 * i : 2 * i + 2] for i in range(lo)], refs[2 * lo :]
    if own_at is not None:
        owns, refs = [refs[2 * i : 2 * i + 2] for i in range(lo)], refs[2 * lo :]
    rights = []
    for _ in range(n_columns):
        rights.append(jnp.concatenate([r[...] for r in refs[: 2 * lo]], axis=0))
        refs = refs[2 * lo :]
    single = lefts[0][0].shape[0] == 1
    for (row, column, _), out in zip(items, refs):
        if row is None:
            odd = ids_ref[own_at] == 1
            left = jnp.concatenate([jnp.where(odd, b[0], a[0]) for a, b in owns], axis=1)
            total = jnp.dot(left, rights[column], preferred_element_type=F32)
            out[...] = total.astype(out.dtype)
            continue
        block = 0 if single else ids_ref[row]
        shard = lefts[0][0].shape[1]
        for p in range(2):
            left = jnp.concatenate([pair[p][block] for pair in lefts], axis=1)
            total = jnp.dot(left, rights[column], preferred_element_type=F32)
            out[p * shard : (p + 1) * shard, :] = total.astype(out.dtype)


def partials(ids, at, items, column_at, lefts, rights, members):
    lo = len(lefts)
    line, part, tokens = lefts[0][0].shape
    shard = part // (lo // 2)
    width = rights[0][0].shape[1] // members
    tile = max(width // 4, 128)
    tiles = width // tile
    single = len({row for row, _, _ in items}) == 1
    if single:
        row = items[0][0]
        left_spec = pl.BlockSpec((1, shard, tokens), lambda i, ids: (ids[row], ids[at["half"]], 0))
    else:
        left_spec = pl.BlockSpec((line, shard, tokens), lambda i, ids: (0, ids[at["half"]], 0))
    flat = [x for pair in lefts for x in pair]
    ins, specs = list(flat), [left_spec] * len(flat)
    own_at = None
    if any(row is None for row, _, _ in items):
        own_at = at["odd"]
        ins += flat
        specs += [
            pl.BlockSpec((1, shard, tokens), lambda i, ids: (ids[at["z"]], ids[at["own"]], 0))
        ] * len(flat)
    for where in column_at:
        ins += [x for pair in rights for x in pair]
        specs += [
            pl.BlockSpec((tokens // 2, tile), lambda i, ids, w=where: (0, ids[w] * tiles + i))
        ] * (2 * lo)
    shapes = [
        jax.ShapeDtypeStruct((shard if row is None else 2 * shard, width), dtype)
        for row, _, dtype in items
    ]
    return pl.pallas_call(
        functools.partial(partials_kernel, lo, items, len(column_at), own_at),
        out_shape=shapes,
        grid_spec=pltpu.PrefetchScalarGridSpec(
            num_scalar_prefetch=1,
            grid=(tiles,),
            in_specs=specs,
            out_specs=[pl.BlockSpec((s.shape[0], tile), lambda i, ids: (0, i)) for s in shapes],
        ),
        compiler_params=pltpu.CompilerParams(vmem_limit_bytes=VMEM_BYTES),
        cost_estimate=SHORT,
    )(ids, *ins)


def slot_kernel(n_pieces, kept, base, ids_ref, *refs):
    pieces, refs = refs[:n_pieces], refs[n_pieces:]
    scaled_refs, refs = refs[:2], refs[2:]
    out_grad_ref, gate_ref, up_ref, in_scale_ref, slot_ref = refs[:5]
    refs = refs[5:]
    if kept:
        before_ref, refs = refs[3], refs[4:]
    grad_gate_ref, grad_up_ref, sum_in_ref, sum_out_ref, weight_ref, sems = refs
    shard = pieces[0].shape[0]

    def copy_of(p):
        start = pl.multiple_of(jnp.maximum(ids_ref[base + 1 + p], 0) * shard, shard)
        return pltpu.make_async_copy(pieces[p], weight_ref.at[pl.ds(start, shard)], sems.at[p])

    for p in range(n_pieces):

        @pl.when(ids_ref[base + 1 + p] >= 0)
        def _():
            copy_of(p).start()

    slot = slot_ref[...]
    gate = gate_ref[...].astype(F32)
    up = up_ref[...].astype(F32)
    tanh = tanh_of(gate)
    cdf = 0.5 * (1.0 + tanh)
    slope = cdf + gate * (0.5 * ROOT_2_PI) * (1.0 - tanh * tanh) * (
        1.0 + (3.0 * CUBIC) * (gate * gate)
    )
    gelu = gate * cdf
    act = gelu * up
    row_in = pick_rows(slot, in_scale_ref[...])
    hidden = (act * row_in).astype(BF16)

    for p in range(n_pieces):

        @pl.when(ids_ref[base + 1 + p] >= 0)
        def _():
            copy_of(p).wait()

    weight = weight_ref[...]
    scaled = jnp.concatenate([r[...] for r in scaled_refs], axis=0)
    grad_hidden = lax.dot_general(
        scaled, weight, (((1,), (1,)), ((), ())), preferred_element_type=F32
    )
    grad_act = grad_hidden * row_in
    grad_gate_ref[...] = (grad_act * up * slope).astype(BF16)
    grad_up_ref[...] = (grad_act * gelu).astype(BF16)
    product = grad_hidden * act
    forward = jnp.dot(hidden, weight, preferred_element_type=F32)
    forward = forward * out_grad_ref[...].astype(F32)
    for k in range(in_scale_ref.shape[0]):
        mine = slot == k
        row = slice(k, k + 1)
        sum_in_ref[row, :] = jnp.sum(jnp.where(mine, product, 0.0), axis=0, keepdims=True)
        more = jnp.sum(jnp.where(mine, forward, 0.0), axis=0, keepdims=True)
        sum_out_ref[row, :] = before_ref[row, :] + more if kept else more


def weight_slot(ids, base, pieces, width, scaled, out_grad, gate, up, in_scale, slot, kept):
    tokens, ff = gate.shape
    d = out_grad.shape[1]
    mem = in_scale.shape[0]
    column = lambda rows: pl.BlockSpec((rows, width), lambda i, ids: (0, ids[base]))
    full = lambda shape: pl.BlockSpec(shape, lambda i, ids: (0, 0))
    anywhere = pl.BlockSpec(memory_space=pl.ANY)
    ins = list(pieces) + list(scaled) + [out_grad, gate, up, in_scale, slot]
    specs = [anywhere] * len(pieces) + [full((tokens // 2, d))] * 2
    specs += [full((tokens, d)), column(tokens), column(tokens), column(mem), full((tokens, 1))]
    aliases = {}
    if kept is not None:
        aliases = {1 + len(ins) + i: i for i in range(3)}
        ins += list(kept)
        specs += [anywhere] * 3 + [full((mem, d))]
    return pl.pallas_call(
        functools.partial(slot_kernel, len(pieces), kept is not None, base),
        out_shape=[
            jax.ShapeDtypeStruct((tokens, ff), BF16),
            jax.ShapeDtypeStruct((tokens, ff), BF16),
            jax.ShapeDtypeStruct((mem, ff), F32),
            jax.ShapeDtypeStruct((mem, d), F32),
        ],
        grid_spec=pltpu.PrefetchScalarGridSpec(
            num_scalar_prefetch=1,
            grid=(1,),
            in_specs=specs,
            out_specs=[column(tokens), column(tokens), column(mem), full((mem, d))],
            scratch_shapes=[
                pltpu.VMEM((width, d), BF16),
                pltpu.SemaphoreType.DMA((len(pieces),)),
            ],
        ),
        input_output_aliases=aliases,
        compiler_params=pltpu.CompilerParams(vmem_limit_bytes=VMEM_BYTES),
        cost_estimate=SHORT,
    )(ids, *ins)


def on_device(groups, members, fsdp):
    def run(gate, up, out_grad, in_scale, out_scale, weight, member_slot):
        tokens, ff = gate.shape
        shard = weight.shape[0]
        columns = out_grad.shape[1] // members
        lo = max(128 // math.gcd(shard, 128), 2)
        line, nh = fsdp // lo, lo // 2
        assert groups == 2 and line * lo == fsdp and line > 1
        width = lo * shard
        group = lax.axis_index("groups")
        member = lax.axis_index("member")
        place_id = lax.axis_index("fsdp")
        z, core = place_id // lo, lax.rem(place_id, lo)
        lower, rising = z < line // 2, core < nh
        slot = member_slot[:, None]
        last = [slot]
        chips = range(line)
        halves = range(nh)

        def after(x):
            return lax.optimization_barrier((x, last[-1]))[0]

        def mark(x):
            last.append(x[0] if isinstance(x, (list, tuple)) else x)
            return x

        def dev(zz, c, outer=0):
            return (outer * line + zz) * lo + c

        def line_step(x, rises, falls):
            pairs = [(dev(a, i), dev(a + 1, i)) for a in rises for i in halves]
            pairs += [(dev(a, nh + i), dev(a - 1, nh + i)) for a in falls for i in halves]
            return lax.ppermute(x, "fsdp", pairs)

        def to_chip(x, sources, o):
            return lax.ppermute(
                x, "fsdp", [(dev(a, c), dev(a, (c + o) % lo)) for a in chips for c in sources(a)]
            )

        every = lambda a: range(lo)

        arrived, mine, twin = [None] * line, [None] * line, [None] * line
        mine_in, twin_in = [None] * line, [None] * line

        def weight_first():
            pairs = []
            for g in range(2):
                for a in chips:
                    for i in halves:
                        if a + 1 < line:
                            pairs.append((dev(a, g * nh + i, g), dev(a + 1, i, g)))
                        if a > 0:
                            pairs.append((dev(a, (1 - g) * nh + i, g), dev(a - 1, nh + i, g)))
            arrived[1] = lax.ppermute(weight, ("groups", "fsdp"), pairs)

        def weight_next(s):
            arrived[s] = line_step(
                after(arrived[s - 1]), range(s - 1, line - 1), range(1, line - s + 1)
            )

        def falls(a, j):
            return a + j < line if a < line // 2 else a < j

        def fell(j):
            table = [int(falls(a, j)) for a in chips]
            flag = jnp.int32(table[-1])
            for a in range(line - 1):
                flag = jnp.where(z == a, table[a], flag)
            return flag

        def holders(j):
            return lambda a: [nh * falls(a, j) + i for i in halves]

        def weight_mine(j):
            block = after(arrived[j])
            if 2 * j > line:
                straight = jnp.where(lower, z + j < line, z >= j)
                block = mark(jnp.where(straight, block, arrived[line - j]))
            mine[j] = block
            pairs = [
                (dev(a, h, g), dev(a, h, 1 - g))
                for g in range(2)
                for a in chips
                for h in holders(j)(a)
            ]
            twin[j] = lax.ppermute(block, ("groups", "fsdp"), pairs)

        def spread_mine(j):
            mine_in[j] = [to_chip(after(mine[j]), holders(j), o) for o in range(1, lo)]

        def spread_twin(j):
            twin_in[j] = [to_chip(after(twin[j]), holders(j), o) for o in range(1, lo)]

        numbers, at = [], {}

        def number(name, value):
            at[name] = len(numbers)
            numbers.append(jnp.asarray(value, jnp.int32))

        number("z", z)
        number("half", lax.rem(core, nh) if nh > 1 else 0)
        number("own", core // 2)
        number("odd", lax.rem(core, 2))
        for j in range(members):
            number(("to", j), lax.rem(member + members - j, members))
        for k in range(1, line):
            number(("send", k), lax.rem(jnp.where(lower, z - k, z + k) + line, line))
            onward = jnp.where(rising, z + line - k, z - line + k)
            number(("keep", k), jnp.clip(onward, 0, line - 1))
        source = [lax.rem(core + lo - o, lo) for o in range(lo)]
        for j in range(line):
            number(("slot", j), lax.rem(jnp.where(lower, z + j, z - j) + line, line))
            if j == 0:
                places = source
            else:
                down = fell(j)
                held = [(h // nh) == down for h in source]
                first = jnp.where(down == 1, 1 - group, group)
                places = [jnp.where(ok, first * nh + h % nh, -1) for ok, h in zip(held, source)]
                places += [
                    jnp.where(ok, (1 - first) * nh + h % nh, -1) for ok, h in zip(held, source)
                ]
            for p, value in enumerate(places):
                number(("piece", j, p), value)
        ids = jnp.stack(numbers)

        kept = [None]

        def use_weight(j):
            if j == 0:
                pieces = [weight] + own_in
            else:
                pieces = [mine[j]] + mine_in[j] + [twin[j]] + twin_in[j]
            kept[0] = mark(
                weight_slot(
                    ids,
                    at[("slot", j)],
                    after(pieces),
                    width,
                    scaled,
                    out_grad,
                    gate,
                    up,
                    in_scale,
                    slot,
                    kept[0],
                )
            )

        weight_first()
        made = mark(prepare(gate, up, in_scale, out_grad, out_scale, slot, line, nh))
        turned, scaled = list(made[:2]), list(made[2:])
        lefts, rights = [turned], [scaled]
        for o in range(1, lo):
            rights.append([to_chip(x, every, o) for x in scaled])
            lefts.append([to_chip(x, every, o) for x in turned])

        got = [None] * line

        def works(a, c, k):
            if k == 0:
                return True
            if a < line // 2:
                return (c < nh) == (k > a)
            return (c >= nh) == (k > line - 1 - a)

        def exchange(k, blocks):
            got[k] = []
            for j in range(1, members):
                pairs = [
                    (dev(a, c, (m + j) % members), dev(a, c, m))
                    for m in range(members)
                    for a in chips
                    for c in range(lo)
                    if works(a, c, k)
                ]
                got[k].append(lax.ppermute(blocks[j - 1], ("member", "fsdp"), pairs))

        others = [at[("to", j)] for j in range(1, members)]
        items = [(at[("send", 1)], j, BF16) for j in range(members - 1)]
        mark(arrived[1])
        made = partials(after(ids), at, items, others, lefts, rights, members)
        mark(made)
        exchange(1, made)
        if line > 2:
            weight_next(2)
        weight_mine(1)
        spread_mine(1)
        own_in = [to_chip(after(weight), every, o) for o in range(1, lo)]
        order = list(range(2, line)) + [0]
        items = []
        for k in order:
            row = at[("send", k)] if k else None
            items += [(row, j, BF16) for j in range(1, members)]
        for k in order:
            row = at[("keep", k)] if k else None
            items.append((row, 0, BF16 if k else F32))
        items.append((at[("keep", 1)], 0, BF16))
        made = mark(
            partials(ids, at, items, [at[("to", 0)]] + others, after(lefts), rights, members)
        )
        to_send = {
            k: made[n * (members - 1) : (n + 1) * (members - 1)] for n, k in enumerate(order)
        }
        sums = dict(zip(order + [1], made[len(order) * (members - 1) :]))

        coming = []

        def line_both(s):
            total = sums[s].astype(F32)
            for one, two in zip(after(got[s]), got[line - s] or got[s]):
                if 2 * s > line:
                    one = jnp.where(rising != lower, two, one)
                total = total + one.astype(F32)
            for x in coming:
                total = total + jnp.concatenate([x[:, :columns], x[:, columns:]]).astype(F32)
            total = total.astype(BF16)
            total = jnp.concatenate([total[:shard], total[shard:]], axis=1)
            rises = [a for a in range(s)]
            falls = [a for a in range(line - s, line)]
            if s + 2 < line and total.shape == weight.shape:
                hop = jnp.where(rising, z > s, z < line - 1 - s)
                total = mark(jnp.where(hop, after(arrived[s + 1]), total))
                rises += range(s + 1, line - 1)
                falls += range(1, line - 1 - s)
                arrived[s + 2] = line_step(total, rises, falls)
                coming[:] = [arrived[s + 2]]
                return
            if s + 2 < line:
                weight_next(s + 2)
            coming[:] = [line_step(mark(total), rises, falls)]

        for s in range(1, line):
            mark(after(got[s]))
            k = s + 1 if s + 1 < line else 0
            exchange(k, after(to_send[k]))
            if s + 1 < line:
                weight_mine(s + 1)
            line_both(s)
            spread_twin(s)
            use_weight(s - 1)
            if s + 1 < line:
                spread_mine(s + 1)
        mark(after(got[0]))
        use_weight(line - 1)
        both = jnp.concatenate(kept[0][2:], axis=1)
        if fsdp & (fsdp - 1):
            both = lax.psum(both, "fsdp")
        else:
            stage = 1
            while stage < fsdp:
                both = both + lax.ppermute(both, "fsdp", [(i, i ^ stage) for i in range(fsdp)])
                stage *= 2
        top, bottom = coming[0][:, :columns], coming[0][:, columns:]
        landed = []
        for part in range(2):
            pairs = [(i, 2 * i + part) for i in halves]
            pairs += [(nh + i, 2 * i + 1 - part) for i in halves]
            x = jnp.where(rising, bottom, top) if part else jnp.where(rising, top, bottom)
            if any(c != d for c, d in pairs):
                x = lax.ppermute(
                    x, "fsdp", [(dev(a, c), dev(a, d)) for a in chips for c, d in pairs]
                )
            landed.append(x)
        grad_down = sums[0]
        for x in got[0] + landed:
            grad_down = grad_down + x.astype(F32)
        return kept[0][0], kept[0][1], grad_down, both[:, :ff], both[:, ff:]

    return run


def solution(mesh):
    rows = P(("groups", "member", "fsdp"), None)
    in_specs = (
        rows,
        rows,
        rows,
        P("member", None),
        P("member", None),
        P("fsdp", None),
        P(("groups", "member", "fsdp")),
    )
    out_specs = (
        rows,
        rows,
        P(("groups", "fsdp"), "member"),
        P(("groups", "member"), None),
        P(("groups", "member"), None),
    )
    run = on_device(mesh.shape["groups"], mesh.shape["member"], mesh.shape["fsdp"])
    return jax.shard_map(run, mesh=mesh, in_specs=in_specs, out_specs=out_specs, check_vma=False)
```

```python
import functools
import math

import jax
import jax.numpy as jnp
from jax import lax
from jax.experimental import pallas as pl
from jax.experimental.pallas import tpu as pltpu
from jax.sharding import PartitionSpec as P

F32 = jnp.float32
BF16 = jnp.bfloat16
VMEM_BYTES = 60 * 1024 * 1024
ROOT_2_PI = math.sqrt(2.0 / math.pi)
CUBIC = 0.044715
SHORT = pl.CostEstimate(flops=1, bytes_accessed=1, transcendentals=0)


def tanh_of(x):
    return jnp.tanh(ROOT_2_PI * (x + CUBIC * (x * x * x)))


def pick_rows(slot, scale):
    rows = jnp.zeros((slot.shape[0], scale.shape[1]), F32)
    for k in range(scale.shape[0]):
        rows = jnp.where(slot == k, scale[k : k + 1, :], rows)
    return rows


def prepare_kernel(nh, gate_ref, up_ref, in_scale_ref, grad_ref, out_scale_ref, slot_ref, *outs):
    slot = slot_ref[...]
    gate = gate_ref[...].astype(F32)
    gelu = gate * (0.5 * (1.0 + tanh_of(gate)))
    act = gelu * up_ref[...].astype(F32)
    turned = (act * pick_rows(slot, in_scale_ref[...])).T.astype(BF16)
    shard = outs[0].shape[1] // nh
    for i in range(nh):
        for p in range(2):
            first = (2 * i + p) * shard
            outs[p][0, i * shard : (i + 1) * shard, :] = turned[first : first + shard]
    scaled = (grad_ref[...].astype(F32) * pick_rows(slot, out_scale_ref[...])).astype(BF16)
    half = scaled.shape[0] // 2
    outs[2][...] = scaled[:half]
    outs[3][...] = scaled[half:]


def prepare(gate, up, in_scale, out_grad, out_scale, slot, blocks, nh):
    tokens, ff = gate.shape
    d = out_grad.shape[1]
    width, columns = ff // blocks, d // blocks
    mem = in_scale.shape[0]
    spec = lambda shape: pl.BlockSpec(shape, lambda i: (0, i))
    turned = jax.ShapeDtypeStruct((blocks, width // 2, tokens), BF16)
    scaled = jax.ShapeDtypeStruct((tokens // 2, d), BF16)
    return pl.pallas_call(
        functools.partial(prepare_kernel, nh),
        out_shape=[turned, turned, scaled, scaled],
        grid=(blocks,),
        in_specs=[
            spec((tokens, width)),
            spec((tokens, width)),
            spec((mem, width)),
            spec((tokens, columns)),
            spec((mem, columns)),
            pl.BlockSpec((tokens, 1), lambda i: (0, 0)),
        ],
        out_specs=[pl.BlockSpec((1, width // 2, tokens), lambda i: (i, 0, 0))] * 2
        + [spec((tokens // 2, columns))] * 2,
        compiler_params=pltpu.CompilerParams(vmem_limit_bytes=VMEM_BYTES),
        cost_estimate=SHORT,
    )(gate, up, in_scale, out_grad, out_scale, slot)


def partials_kernel(lo, items, n_columns, own_at, ids_ref, *refs):
    lefts, refs = [refs[2 * i : 2 * i + 2] for i in range(lo)], refs[2 * lo :]
    if own_at is not None:
        owns, refs = [refs[2 * i : 2 * i + 2] for i in range(lo)], refs[2 * lo :]
    rights = []
    for _ in range(n_columns):
        rights.append(jnp.concatenate([r[...] for r in refs[: 2 * lo]], axis=0))
        refs = refs[2 * lo :]
    single = lefts[0][0].shape[0] == 1
    for (row, column, _), out in zip(items, refs):
        if row is None:
            odd = ids_ref[own_at] == 1
            left = jnp.concatenate([jnp.where(odd, b[0], a[0]) for a, b in owns], axis=1)
            total = jnp.dot(left, rights[column], preferred_element_type=F32)
            out[...] = total.astype(out.dtype)
            continue
        block = 0 if single else ids_ref[row]
        shard = lefts[0][0].shape[1]
        for p in range(2):
            left = jnp.concatenate([pair[p][block] for pair in lefts], axis=1)
            total = jnp.dot(left, rights[column], preferred_element_type=F32)
            out[p * shard : (p + 1) * shard, :] = total.astype(out.dtype)


def partials(ids, at, items, column_at, lefts, rights, members):
    lo = len(lefts)
    line, part, tokens = lefts[0][0].shape
    shard = part // (lo // 2)
    width = rights[0][0].shape[1] // members
    tile = max(width // 4, 128)
    tiles = width // tile
    single = len({row for row, _, _ in items}) == 1
    if single:
        row = items[0][0]
        left_spec = pl.BlockSpec((1, shard, tokens), lambda i, ids: (ids[row], ids[at["half"]], 0))
    else:
        left_spec = pl.BlockSpec((line, shard, tokens), lambda i, ids: (0, ids[at["half"]], 0))
    flat = [x for pair in lefts for x in pair]
    ins, specs = list(flat), [left_spec] * len(flat)
    own_at = None
    if any(row is None for row, _, _ in items):
        own_at = at["odd"]
        ins += flat
        specs += [
            pl.BlockSpec((1, shard, tokens), lambda i, ids: (ids[at["z"]], ids[at["own"]], 0))
        ] * len(flat)
    for where in column_at:
        ins += [x for pair in rights for x in pair]
        specs += [
            pl.BlockSpec((tokens // 2, tile), lambda i, ids, w=where: (0, ids[w] * tiles + i))
        ] * (2 * lo)
    shapes = [
        jax.ShapeDtypeStruct((shard if row is None else 2 * shard, width), dtype)
        for row, _, dtype in items
    ]
    return pl.pallas_call(
        functools.partial(partials_kernel, lo, items, len(column_at), own_at),
        out_shape=shapes,
        grid_spec=pltpu.PrefetchScalarGridSpec(
            num_scalar_prefetch=1,
            grid=(tiles,),
            in_specs=specs,
            out_specs=[pl.BlockSpec((s.shape[0], tile), lambda i, ids: (0, i)) for s in shapes],
        ),
        compiler_params=pltpu.CompilerParams(vmem_limit_bytes=VMEM_BYTES),
        cost_estimate=SHORT,
    )(ids, *ins)


def hop_kernel(n_got, either, n_coming, flags, ids_ref, sum_ref, *refs):
    gots, refs = refs[: n_got * (1 + either)], refs[n_got * (1 + either) :]
    out_ref = refs[-1]
    total = sum_ref[...].astype(F32)
    for i in range(n_got):
        one = gots[i][...].astype(F32)
        if either:
            one = jnp.where(ids_ref[flags[0]] == 1, gots[n_got + i][...].astype(F32), one)
        total = total + one
    for i in range(n_coming):
        total = total + refs[i][...].astype(F32)
    if len(refs) > n_coming + 1:
        total = jnp.where(ids_ref[flags[1]] == 1, refs[n_coming][...].astype(F32), total)
    out_ref[...] = total.astype(BF16)


def hop(ids, flags, own, got, other, coming, weight):
    rows, columns = own.shape
    stacked = pl.BlockSpec((rows // 2, columns), lambda i, ids: (i, 0))
    beside = pl.BlockSpec((rows // 2, columns), lambda i, ids: (0, i))
    ins = [own] + got + other + coming + weight
    return pl.pallas_call(
        functools.partial(hop_kernel, len(got), bool(other), len(coming), flags),
        out_shape=jax.ShapeDtypeStruct((rows // 2, 2 * columns), BF16),
        grid_spec=pltpu.PrefetchScalarGridSpec(
            num_scalar_prefetch=1,
            grid=(2,),
            in_specs=[stacked] * (1 + len(got) + len(other))
            + [beside] * (len(coming) + len(weight)),
            out_specs=beside,
        ),
        compiler_params=pltpu.CompilerParams(vmem_limit_bytes=VMEM_BYTES),
        cost_estimate=SHORT,
    )(ids, *ins)


def slot_kernel(n, lo, kept, base, ids_ref, *refs):
    pieces, refs = refs[: n * lo], refs[n * lo :]
    scaled_refs, refs = refs[:2], refs[2:]
    out_grad_ref, gate_ref, up_ref, in_scale_ref, slot_ref = refs[:5]
    refs = refs[5:]
    if kept:
        before_ref, refs = refs[3], refs[4:]
    grad_gate_ref, grad_up_ref, sum_in_ref, sum_out_ref, weight_ref, sems = refs
    shard = pieces[0].shape[0]

    step = pl.program_id(0)

    def copy_of(i, p):
        start = pl.multiple_of(ids_ref[base + i * (lo + 1) + 1 + p] * shard, shard)
        return pltpu.make_async_copy(
            pieces[i * lo + p], weight_ref.at[i, pl.ds(start, shard)], sems.at[i, p]
        )

    @pl.when(step == 0)
    def _():
        for i in range(n):
            for p in range(lo):
                copy_of(i, p).start()

    slot = slot_ref[...]
    gate = gate_ref[...].astype(F32)
    up = up_ref[...].astype(F32)
    tanh = tanh_of(gate)
    cdf = 0.5 * (1.0 + tanh)
    slope = cdf + gate * (0.5 * ROOT_2_PI) * (1.0 - tanh * tanh) * (
        1.0 + (3.0 * CUBIC) * (gate * gate)
    )
    gelu = gate * cdf
    act = gelu * up
    row_in = pick_rows(slot, in_scale_ref[...])
    hidden = (act * row_in).astype(BF16)

    for i in range(n):

        @pl.when(step == i)
        def _():
            for p in range(lo):
                copy_of(i, p).wait()

    weight = weight_ref[step]
    scaled = jnp.concatenate([r[...] for r in scaled_refs], axis=0)
    grad_hidden = lax.dot_general(
        scaled, weight, (((1,), (1,)), ((), ())), preferred_element_type=F32
    )
    grad_act = grad_hidden * row_in
    grad_gate_ref[...] = (grad_act * up * slope).astype(BF16)
    grad_up_ref[...] = (grad_act * gelu).astype(BF16)
    product = grad_hidden * act
    forward = jnp.dot(hidden, weight, preferred_element_type=F32)
    forward = forward * out_grad_ref[...].astype(F32)
    mores = []
    for k in range(in_scale_ref.shape[0]):
        mine = slot == k
        row = slice(k, k + 1)
        sum_in_ref[row, :] = jnp.sum(jnp.where(mine, product, 0.0), axis=0, keepdims=True)
        more = jnp.sum(jnp.where(mine, forward, 0.0), axis=0, keepdims=True)
        mores.append(more)

    @pl.when(step == 0)
    def _():
        for k, more in enumerate(mores):
            row = slice(k, k + 1)
            sum_out_ref[row, :] = before_ref[row, :] + more if kept else more

    @pl.when(step > 0)
    def _():
        for k, more in enumerate(mores):
            row = slice(k, k + 1)
            sum_out_ref[row, :] = sum_out_ref[row, :] + more


def weight_slots(ids, base, lo, pieces, width, scaled, out_grad, gate, up, in_scale, slot, kept):
    tokens, ff = gate.shape
    d = out_grad.shape[1]
    mem = in_scale.shape[0]
    n = len(pieces) // lo
    column = lambda rows: pl.BlockSpec(
        (rows, width), lambda i, ids: (0, ids[base + i * (lo + 1)])
    )
    full = lambda shape: pl.BlockSpec(shape, lambda i, ids: (0, 0))
    anywhere = pl.BlockSpec(memory_space=pl.ANY)
    ins = list(pieces) + list(scaled) + [out_grad, gate, up, in_scale, slot]
    specs = [anywhere] * len(pieces) + [full((tokens // 2, d))] * 2
    specs += [full((tokens, d)), column(tokens), column(tokens), column(mem), full((tokens, 1))]
    aliases = {}
    if kept is not None:
        aliases = {1 + len(ins) + i: i for i in range(3)}
        ins += list(kept)
        specs += [anywhere] * 3 + [full((mem, d))]
    return pl.pallas_call(
        functools.partial(slot_kernel, n, lo, kept is not None, base),
        out_shape=[
            jax.ShapeDtypeStruct((tokens, ff), BF16),
            jax.ShapeDtypeStruct((tokens, ff), BF16),
            jax.ShapeDtypeStruct((mem, ff), F32),
            jax.ShapeDtypeStruct((mem, d), F32),
        ],
        grid_spec=pltpu.PrefetchScalarGridSpec(
            num_scalar_prefetch=1,
            grid=(n,),
            in_specs=specs,
            out_specs=[column(tokens), column(tokens), column(mem), full((mem, d))],
            scratch_shapes=[
                pltpu.VMEM((n, width, d), BF16),
                pltpu.SemaphoreType.DMA((n, lo)),
            ],
        ),
        input_output_aliases=aliases,
        compiler_params=pltpu.CompilerParams(vmem_limit_bytes=VMEM_BYTES),
        cost_estimate=SHORT,
    )(ids, *ins)


def on_device(groups, members, fsdp):
    def run(gate, up, out_grad, in_scale, out_scale, weight, member_slot):
        tokens, ff = gate.shape
        shard = weight.shape[0]
        columns = out_grad.shape[1] // members
        lo = max(128 // math.gcd(shard, 128), 2)
        line, nh = fsdp // lo, lo // 2
        assert groups == 2 and line * lo == fsdp and line > 1
        width = lo * shard
        group = lax.axis_index("groups")
        member = lax.axis_index("member")
        place_id = lax.axis_index("fsdp")
        z, core = place_id // lo, lax.rem(place_id, lo)
        lower, rising = z < line // 2, core < nh
        slot = member_slot[:, None]
        chips = range(line)
        halves = range(nh)

        def tie(x, y):
            return lax.optimization_barrier((x, y))

        def dev(zz, c, outer=0):
            return (outer * line + zz) * lo + c

        def line_step(x, rises, falls):
            pairs = [(dev(a, i), dev(a + 1, i)) for a in rises for i in halves]
            pairs += [(dev(a, nh + i), dev(a - 1, nh + i)) for a in falls for i in halves]
            return lax.ppermute(x, "fsdp", pairs)

        def to_chip(x, sources, o):
            return lax.ppermute(
                x, "fsdp", [(dev(a, c), dev(a, (c + o) % lo)) for a in chips for c in sources(a)]
            )

        every = lambda a: range(lo)

        arrived, mine, twin = [None] * line, [None] * line, [None] * line
        whole = [None] * line

        def weight_first():
            pairs = []
            for g in range(2):
                for a in chips:
                    for i in halves:
                        if a + 1 < line:
                            pairs.append((dev(a, g * nh + i, g), dev(a + 1, i, g)))
                        if a > 0:
                            pairs.append((dev(a, (1 - g) * nh + i, g), dev(a - 1, nh + i, g)))
            arrived[1] = lax.ppermute(weight, ("groups", "fsdp"), pairs)

        def weight_next(s):
            arrived[s] = line_step(
                arrived[s - 1], range(s - 1, line - 1), range(1, line - s + 1)
            )

        def falls(a, j):
            return a + j < line if a < line // 2 else a < j

        def fell(j):
            table = [int(falls(a, j)) for a in chips]
            flag = jnp.int32(table[-1])
            for a in range(line - 1):
                flag = jnp.where(z == a, table[a], flag)
            return flag

        def holders(j):
            return lambda a: [nh * falls(a, j) + i for i in halves]

        def weight_mine(j):
            block = arrived[j]
            if 2 * j > line:
                straight = jnp.where(lower, z + j < line, z >= j)
                block = jnp.where(straight, block, arrived[line - j])
            mine[j] = block
            pairs = [
                (dev(a, h, g), dev(a, (h + nh) % lo, 1 - g))
                for g in range(2)
                for a in chips
                for h in holders(j)(a)
            ]
            twin[j] = lax.ppermute(block, ("groups", "fsdp"), pairs)

        def spread(j, core):
            held = jnp.where((core >= nh) == (fell(j) == 1), mine[j], twin[j])
            whole[j] = [held] + [to_chip(held, every, o) for o in range(1, lo)]

        numbers, at = [], {}

        def number(name, value):
            at[name] = len(numbers)
            numbers.append(jnp.asarray(value, jnp.int32))

        number("z", z)
        number("half", lax.rem(core, nh) if nh > 1 else 0)
        number("own", core // 2)
        number("odd", lax.rem(core, 2))
        number("other", rising != lower)
        for s in range(1, line):
            number(("hop", s), jnp.where(rising, z > s, z < line - 1 - s))
        for j in range(members):
            number(("to", j), lax.rem(member + members - j, members))
        for k in range(1, line):
            number(("send", k), lax.rem(jnp.where(lower, z - k, z + k) + line, line))
            onward = jnp.where(rising, z + line - k, z - line + k)
            number(("keep", k), jnp.clip(onward, 0, line - 1))
        source = [lax.rem(core + lo - o, lo) for o in range(lo)]
        for j in range(line):
            number(("slot", j), lax.rem(jnp.where(lower, z + j, z - j) + line, line))
            if j == 0:
                places = source
            else:
                down = fell(j)
                first = jnp.where(down == 1, 1 - group, group)
                places = [
                    jnp.where((h // nh) == down, first, 1 - first) * nh + h % nh for h in source
                ]
            for p, value in enumerate(places):
                number(("piece", j, p), value)
        ids = jnp.stack(numbers)

        kept = [None]

        def use_weight(first, n, ids):
            kept[0] = weight_slots(
                ids,
                at[("slot", first)],
                lo,
                [x for j in range(first, first + n) for x in whole[j]],
                width,
                scaled,
                out_grad,
                gate,
                up,
                in_scale,
                slot,
                kept[0],
            )

        weight_first()
        made = prepare(gate, up, in_scale, out_grad, out_scale, slot, line, nh)
        turned, scaled = list(made[:2]), list(made[2:])
        lefts, rights = [turned], [scaled]
        for o in range(1, lo):
            rights.append([to_chip(x, every, o) for x in scaled])
            lefts.append([to_chip(x, every, o) for x in turned])

        got = [None] * line

        def works(a, c, k):
            if k == 0:
                return True
            if a < line // 2:
                return (c < nh) == (k > a)
            return (c >= nh) == (k > line - 1 - a)

        def exchange(k, blocks):
            got[k] = []
            for j in range(1, members):
                pairs = [
                    (dev(a, c, (m + j) % members), dev(a, c, m))
                    for m in range(members)
                    for a in chips
                    for c in range(lo)
                    if works(a, c, k)
                ]
                got[k].append(lax.ppermute(blocks[j - 1], ("member", "fsdp"), pairs))

        others = [at[("to", j)] for j in range(1, members)]
        items = [(at[("send", 1)], j, BF16) for j in range(members - 1)]
        ids, arrived[1] = tie(ids, arrived[1])
        made = partials(ids, at, items, others, lefts, rights, members)
        behind = weight
        exchange(1, made)
        if line > 2:
            weight_next(2)
        weight_mine(1)
        whole[0] = [weight] + [to_chip(behind, every, o) for o in range(1, lo)]
        ids, whole[0] = tie(ids, whole[0])
        order = list(range(2, line)) + [0]
        items = []
        for k in order:
            row = at[("send", k)] if k else None
            items += [(row, j, BF16) for j in range(1, members)]
        for k in order:
            row = at[("keep", k)] if k else None
            items.append((row, 0, BF16 if k else F32))
        items.append((at[("keep", 1)], 0, BF16))
        made = partials(ids, at, items, [at[("to", 0)]] + others, lefts, rights, members)
        twin[1], made = tie(twin[1], made)
        to_send = {
            k: made[n * (members - 1) : (n + 1) * (members - 1)] for n, k in enumerate(order)
        }
        sums = dict(zip(order + [1], made[len(order) * (members - 1) :]))

        coming = []
        joint = shard == weight.shape[0] and columns * 2 == weight.shape[1]

        def line_sum(s):
            return hop(
                ids,
                (at["other"], at[("hop", s)]),
                sums[s],
                list(got[s]),
                list(got[line - s]) if 2 * s > line else [],
                list(coming),
                [arrived[s + 1]] if s + 2 < line and joint else [],
            )

        def line_send(s, total):
            rises, falls = list(range(s)), list(range(line - s, line))
            if s + 2 < line and joint:
                rises += range(s + 1, line - 1)
                falls += range(1, line - 1 - s)
                arrived[s + 2] = line_step(total, rises, falls)
                coming[:] = [arrived[s + 2]]
                return
            coming[:] = [line_step(total, rises, falls)]
            if s + 2 < line:
                weight_next(s + 2)

        spread(1, core)
        whole[1][0], got[1] = tie(whole[1][0], got[1])
        for s in range(1, line):
            k = s + 1 if s + 1 < line else 0
            to_send[k], got[s] = tie(to_send[k], got[s])
            total = line_sum(s)
            ids, total = tie(ids, total)
            here, total = tie(core, total)
            line_send(s, total)
            exchange(k, to_send[k])
            if s + 1 < line:
                weight_mine(s + 1)
            if s > 1:
                spread(s, here)
            first = s if s > 1 else 0
            use_weight(first, s + 1 - first, ids)
            if s + 1 < line:
                (got[k], coming[0]), kept[0] = tie((got[k], coming[0]), kept[0])
                twin[s + 1], kept[0] = tie(twin[s + 1], kept[0])
                if s + 2 < line and joint:
                    arrived[s + 2] = coming[0]
        both = jnp.concatenate(kept[0][2:], axis=1)
        if fsdp & (fsdp - 1):
            both = lax.psum(both, "fsdp")
        else:
            stage = 1
            while stage < fsdp:
                if 2 * stage == fsdp:
                    got[0], both = tie(got[0], both)
                    coming[0], both = tie(coming[0], both)
                both = both + lax.ppermute(both, "fsdp", [(i, i ^ stage) for i in range(fsdp)])
                stage *= 2
        top, bottom = coming[0][:, :columns], coming[0][:, columns:]
        landed = []
        for part in range(2):
            pairs = [(i, 2 * i + part) for i in halves]
            pairs += [(nh + i, 2 * i + 1 - part) for i in halves]
            x = jnp.where(rising, bottom, top) if part else jnp.where(rising, top, bottom)
            if any(c != d for c, d in pairs):
                x = lax.ppermute(
                    x, "fsdp", [(dev(a, c), dev(a, d)) for a in chips for c, d in pairs]
                )
            landed.append(x)
        grad_down = sums[0]
        for x in got[0] + landed:
            grad_down = grad_down + x.astype(F32)
        return kept[0][0], kept[0][1], grad_down, both[:, :ff], both[:, ff:]

    return run


def solution(mesh):
    rows = P(("groups", "member", "fsdp"), None)
    in_specs = (
        rows,
        rows,
        rows,
        P("member", None),
        P("member", None),
        P("fsdp", None),
        P(("groups", "member", "fsdp")),
    )
    out_specs = (
        rows,
        rows,
        P(("groups", "fsdp"), "member"),
        P(("groups", "member"), None),
        P(("groups", "member"), None),
    )
    run = on_device(mesh.shape["groups"], mesh.shape["member"], mesh.shape["fsdp"])
    return jax.shard_map(run, mesh=mesh, in_specs=in_specs, out_specs=out_specs, check_vma=False)
```

```python
import functools
import math

import jax
import jax.numpy as jnp
from jax import lax
from jax.experimental import pallas as pl
from jax.experimental.pallas import tpu as pltpu
from jax.sharding import PartitionSpec as P

F32 = jnp.float32
BF16 = jnp.bfloat16
VMEM_BYTES = 60 * 1024 * 1024
ROOT_2_PI = math.sqrt(2.0 / math.pi)
CUBIC = 0.044715
SHORT = pl.CostEstimate(flops=1, bytes_accessed=1, transcendentals=0)


def tanh_of(x):
    return jnp.tanh(ROOT_2_PI * (x + CUBIC * (x * x * x)))


def pick_rows(slot, scale):
    rows = jnp.zeros((slot.shape[0], scale.shape[1]), F32)
    for k in range(scale.shape[0]):
        rows = jnp.where(slot == k, scale[k : k + 1, :], rows)
    return rows


def prepare_kernel(nh, gate_ref, up_ref, in_scale_ref, grad_ref, out_scale_ref, slot_ref, *outs):
    slot = slot_ref[...]
    gate = gate_ref[...].astype(F32)
    gelu = gate * (0.5 * (1.0 + tanh_of(gate)))
    act = gelu * up_ref[...].astype(F32)
    turned = (act * pick_rows(slot, in_scale_ref[...])).T.astype(BF16)
    shard = outs[0].shape[1] // nh
    for i in range(nh):
        for p in range(2):
            first = (2 * i + p) * shard
            outs[p][0, i * shard : (i + 1) * shard, :] = turned[first : first + shard]
    scaled = (grad_ref[...].astype(F32) * pick_rows(slot, out_scale_ref[...])).astype(BF16)
    half = scaled.shape[0] // 2
    outs[2][...] = scaled[:half]
    outs[3][...] = scaled[half:]


def prepare(gate, up, in_scale, out_grad, out_scale, slot, blocks, nh):
    tokens, ff = gate.shape
    d = out_grad.shape[1]
    width, columns = ff // blocks, d // blocks
    mem = in_scale.shape[0]
    spec = lambda shape: pl.BlockSpec(shape, lambda i: (0, i))
    turned = jax.ShapeDtypeStruct((blocks, width // 2, tokens), BF16)
    scaled = jax.ShapeDtypeStruct((tokens // 2, d), BF16)
    return pl.pallas_call(
        functools.partial(prepare_kernel, nh),
        out_shape=[turned, turned, scaled, scaled],
        grid=(blocks,),
        in_specs=[
            spec((tokens, width)),
            spec((tokens, width)),
            spec((mem, width)),
            spec((tokens, columns)),
            spec((mem, columns)),
            pl.BlockSpec((tokens, 1), lambda i: (0, 0)),
        ],
        out_specs=[pl.BlockSpec((1, width // 2, tokens), lambda i: (i, 0, 0))] * 2
        + [spec((tokens // 2, columns))] * 2,
        compiler_params=pltpu.CompilerParams(vmem_limit_bytes=VMEM_BYTES),
        cost_estimate=SHORT,
    )(gate, up, in_scale, out_grad, out_scale, slot)


def partials_kernel(lo, items, n_columns, own_at, ids_ref, *refs):
    lefts, refs = [refs[2 * i : 2 * i + 2] for i in range(lo)], refs[2 * lo :]
    if own_at is not None:
        owns, refs = [refs[2 * i : 2 * i + 2] for i in range(lo)], refs[2 * lo :]
    rights = []
    for _ in range(n_columns):
        rights.append(jnp.concatenate([r[...] for r in refs[: 2 * lo]], axis=0))
        refs = refs[2 * lo :]
    single = lefts[0][0].shape[0] == 1
    for (row, column, _), out in zip(items, refs):
        if row is None:
            odd = ids_ref[own_at] == 1
            left = jnp.concatenate([jnp.where(odd, b[0], a[0]) for a, b in owns], axis=1)
            total = jnp.dot(left, rights[column], preferred_element_type=F32)
            out[...] = total.astype(out.dtype)
            continue
        block = 0 if single else ids_ref[row]
        shard = lefts[0][0].shape[1]
        for p in range(2):
            left = jnp.concatenate([pair[p][block] for pair in lefts], axis=1)
            total = jnp.dot(left, rights[column], preferred_element_type=F32)
            out[p * shard : (p + 1) * shard, :] = total.astype(out.dtype)


def partials(ids, at, items, column_at, lefts, rights, members):
    lo = len(lefts)
    line, part, tokens = lefts[0][0].shape
    shard = part // (lo // 2)
    width = rights[0][0].shape[1] // members
    tile = max(width // 4, 128)
    tiles = width // tile
    single = len({row for row, _, _ in items}) == 1
    if single:
        row = items[0][0]
        left_spec = pl.BlockSpec((1, shard, tokens), lambda i, ids: (ids[row], ids[at["half"]], 0))
    else:
        left_spec = pl.BlockSpec((line, shard, tokens), lambda i, ids: (0, ids[at["half"]], 0))
    flat = [x for pair in lefts for x in pair]
    ins, specs = list(flat), [left_spec] * len(flat)
    own_at = None
    if any(row is None for row, _, _ in items):
        own_at = at["odd"]
        ins += flat
        specs += [
            pl.BlockSpec((1, shard, tokens), lambda i, ids: (ids[at["z"]], ids[at["own"]], 0))
        ] * len(flat)
    for where in column_at:
        ins += [x for pair in rights for x in pair]
        specs += [
            pl.BlockSpec((tokens // 2, tile), lambda i, ids, w=where: (0, ids[w] * tiles + i))
        ] * (2 * lo)
    shapes = [
        jax.ShapeDtypeStruct((shard if row is None else 2 * shard, width), dtype)
        for row, _, dtype in items
    ]
    return pl.pallas_call(
        functools.partial(partials_kernel, lo, items, len(column_at), own_at),
        out_shape=shapes,
        grid_spec=pltpu.PrefetchScalarGridSpec(
            num_scalar_prefetch=1,
            grid=(tiles,),
            in_specs=specs,
            out_specs=[pl.BlockSpec((s.shape[0], tile), lambda i, ids: (0, i)) for s in shapes],
        ),
        compiler_params=pltpu.CompilerParams(vmem_limit_bytes=VMEM_BYTES),
        cost_estimate=SHORT,
    )(ids, *ins)


def hop_kernel(n_got, either, n_coming, flags, ids_ref, sum_ref, *refs):
    gots, refs = refs[: n_got * (1 + either)], refs[n_got * (1 + either) :]
    out_ref = refs[-1]
    total = sum_ref[...].astype(F32)
    for i in range(n_got):
        one = gots[i][...].astype(F32)
        if either:
            one = jnp.where(ids_ref[flags[0]] == 1, gots[n_got + i][...].astype(F32), one)
        total = total + one
    for i in range(n_coming):
        total = total + refs[i][...].astype(F32)
    if len(refs) > n_coming + 1:
        total = jnp.where(ids_ref[flags[1]] == 1, refs[n_coming][...].astype(F32), total)
    out_ref[...] = total.astype(BF16)


def hop(ids, flags, own, got, other, coming, weight):
    rows, columns = own.shape
    stacked = pl.BlockSpec((rows // 2, columns), lambda i, ids: (i, 0))
    beside = pl.BlockSpec((rows // 2, columns), lambda i, ids: (0, i))
    ins = [own] + got + other + coming + weight
    return pl.pallas_call(
        functools.partial(hop_kernel, len(got), bool(other), len(coming), flags),
        out_shape=jax.ShapeDtypeStruct((rows // 2, 2 * columns), BF16),
        grid_spec=pltpu.PrefetchScalarGridSpec(
            num_scalar_prefetch=1,
            grid=(2,),
            in_specs=[stacked] * (1 + len(got) + len(other))
            + [beside] * (len(coming) + len(weight)),
            out_specs=beside,
        ),
        compiler_params=pltpu.CompilerParams(vmem_limit_bytes=VMEM_BYTES),
        cost_estimate=SHORT,
    )(ids, *ins)


def slot_kernel(n, lo, kept, base, ids_ref, *refs):
    pieces, refs = refs[: n * lo], refs[n * lo :]
    scaled_refs, refs = refs[:2], refs[2:]
    out_grad_ref, gate_ref, up_ref, in_scale_ref, slot_ref = refs[:5]
    refs = refs[5:]
    if kept:
        before_ref, refs = refs[3], refs[4:]
    grad_gate_ref, grad_up_ref, sum_in_ref, sum_out_ref, weight_ref, sems = refs
    shard = pieces[0].shape[0]

    step = pl.program_id(0)

    def copy_of(i, p):
        start = pl.multiple_of(ids_ref[base + i * (lo + 1) + 1 + p] * shard, shard)
        return pltpu.make_async_copy(
            pieces[i * lo + p], weight_ref.at[i, pl.ds(start, shard)], sems.at[i, p]
        )

    @pl.when(step == 0)
    def _():
        for i in range(n):
            for p in range(lo):
                copy_of(i, p).start()

    slot = slot_ref[...]
    gate = gate_ref[...].astype(F32)
    up = up_ref[...].astype(F32)
    tanh = tanh_of(gate)
    cdf = 0.5 * (1.0 + tanh)
    slope = cdf + gate * (0.5 * ROOT_2_PI) * (1.0 - tanh * tanh) * (
        1.0 + (3.0 * CUBIC) * (gate * gate)
    )
    gelu = gate * cdf
    act = gelu * up
    row_in = pick_rows(slot, in_scale_ref[...])
    hidden = (act * row_in).astype(BF16)

    for i in range(n):

        @pl.when(step == i)
        def _():
            for p in range(lo):
                copy_of(i, p).wait()

    weight = weight_ref[step]
    scaled = jnp.concatenate([r[...] for r in scaled_refs], axis=0)
    grad_hidden = lax.dot_general(
        scaled, weight, (((1,), (1,)), ((), ())), preferred_element_type=F32
    )
    grad_act = grad_hidden * row_in
    grad_gate_ref[...] = (grad_act * up * slope).astype(BF16)
    grad_up_ref[...] = (grad_act * gelu).astype(BF16)
    product = grad_hidden * act
    forward = jnp.dot(hidden, weight, preferred_element_type=F32)
    forward = forward * out_grad_ref[...].astype(F32)
    mores = []
    for k in range(in_scale_ref.shape[0]):
        mine = slot == k
        row = slice(k, k + 1)
        sum_in_ref[row, :] = jnp.sum(jnp.where(mine, product, 0.0), axis=0, keepdims=True)
        more = jnp.sum(jnp.where(mine, forward, 0.0), axis=0, keepdims=True)
        mores.append(more)

    @pl.when(step == 0)
    def _():
        for k, more in enumerate(mores):
            row = slice(k, k + 1)
            sum_out_ref[row, :] = before_ref[row, :] + more if kept else more

    @pl.when(step > 0)
    def _():
        for k, more in enumerate(mores):
            row = slice(k, k + 1)
            sum_out_ref[row, :] = sum_out_ref[row, :] + more


def weight_slots(ids, base, lo, pieces, width, scaled, out_grad, gate, up, in_scale, slot, kept):
    tokens, ff = gate.shape
    d = out_grad.shape[1]
    mem = in_scale.shape[0]
    n = len(pieces) // lo
    column = lambda rows: pl.BlockSpec(
        (rows, width), lambda i, ids: (0, ids[base + i * (lo + 1)])
    )
    full = lambda shape: pl.BlockSpec(shape, lambda i, ids: (0, 0))
    anywhere = pl.BlockSpec(memory_space=pl.ANY)
    ins = list(pieces) + list(scaled) + [out_grad, gate, up, in_scale, slot]
    specs = [anywhere] * len(pieces) + [full((tokens // 2, d))] * 2
    specs += [full((tokens, d)), column(tokens), column(tokens), column(mem), full((tokens, 1))]
    aliases = {}
    if kept is not None:
        aliases = {1 + len(ins) + i: i for i in range(3)}
        ins += list(kept)
        specs += [anywhere] * 3 + [full((mem, d))]
    return pl.pallas_call(
        functools.partial(slot_kernel, n, lo, kept is not None, base),
        out_shape=[
            jax.ShapeDtypeStruct((tokens, ff), BF16),
            jax.ShapeDtypeStruct((tokens, ff), BF16),
            jax.ShapeDtypeStruct((mem, ff), F32),
            jax.ShapeDtypeStruct((mem, d), F32),
        ],
        grid_spec=pltpu.PrefetchScalarGridSpec(
            num_scalar_prefetch=1,
            grid=(n,),
            in_specs=specs,
            out_specs=[column(tokens), column(tokens), column(mem), full((mem, d))],
            scratch_shapes=[
                pltpu.VMEM((n, width, d), BF16),
                pltpu.SemaphoreType.DMA((n, lo)),
            ],
        ),
        input_output_aliases=aliases,
        compiler_params=pltpu.CompilerParams(vmem_limit_bytes=VMEM_BYTES),
        cost_estimate=SHORT,
    )(ids, *ins)


def on_device(groups, members, fsdp):
    def run(gate, up, out_grad, in_scale, out_scale, weight, member_slot):
        tokens, ff = gate.shape
        shard = weight.shape[0]
        columns = out_grad.shape[1] // members
        lo = max(128 // math.gcd(shard, 128), 2)
        line, nh = fsdp // lo, lo // 2
        assert groups == 2 and line * lo == fsdp and line > 1
        width = lo * shard
        group = lax.axis_index("groups")
        member = lax.axis_index("member")
        place_id = lax.axis_index("fsdp")
        z, core = place_id // lo, lax.rem(place_id, lo)
        lower, rising = z < line // 2, core < nh
        slot = member_slot[:, None]
        chips = range(line)
        halves = range(nh)

        def tie(x, y):
            return lax.optimization_barrier((x, y))

        def dev(zz, c, outer=0):
            return (outer * line + zz) * lo + c

        def line_step(x, rises, falls):
            pairs = [(dev(a, i), dev(a + 1, i)) for a in rises for i in halves]
            pairs += [(dev(a, nh + i), dev(a - 1, nh + i)) for a in falls for i in halves]
            return lax.ppermute(x, "fsdp", pairs)

        def to_chip(x, sources, o):
            return lax.ppermute(
                x, "fsdp", [(dev(a, c), dev(a, (c + o) % lo)) for a in chips for c in sources(a)]
            )

        every = lambda a: range(lo)

        arrived, mine, twin = [None] * line, [None] * line, [None] * line
        whole = [None] * line

        def weight_first():
            pairs = []
            for g in range(2):
                for a in chips:
                    for i in halves:
                        if a + 1 < line:
                            pairs.append((dev(a, g * nh + i, g), dev(a + 1, i, g)))
                        if a > 0:
                            pairs.append((dev(a, (1 - g) * nh + i, g), dev(a - 1, nh + i, g)))
            arrived[1] = lax.ppermute(weight, ("groups", "fsdp"), pairs)

        def weight_next(s):
            arrived[s] = line_step(
                arrived[s - 1], range(s - 1, line - 1), range(1, line - s + 1)
            )

        def falls(a, j):
            return a + j < line if a < line // 2 else a < j

        def fell(j):
            table = [int(falls(a, j)) for a in chips]
            flag = jnp.int32(table[-1])
            for a in range(line - 1):
                flag = jnp.where(z == a, table[a], flag)
            return flag

        def holders(j):
            return lambda a: [nh * falls(a, j) + i for i in halves]

        def weight_mine(j):
            block = arrived[j]
            if 2 * j > line:
                straight = jnp.where(lower, z + j < line, z >= j)
                block = jnp.where(straight, block, arrived[line - j])
            mine[j] = block
            pairs = [
                (dev(a, h, g), dev(a, (h + nh) % lo, 1 - g))
                for g in range(2)
                for a in chips
                for h in holders(j)(a)
            ]
            twin[j] = lax.ppermute(block, ("groups", "fsdp"), pairs)

        def spread(j, core):
            held = jnp.where((core >= nh) == (fell(j) == 1), mine[j], twin[j])
            whole[j] = [held] + [to_chip(held, every, o) for o in range(1, lo)]

        numbers, at = [], {}

        def number(name, value):
            at[name] = len(numbers)
            numbers.append(jnp.asarray(value, jnp.int32))

        number("z", z)
        number("half", lax.rem(core, nh) if nh > 1 else 0)
        number("own", core // 2)
        number("odd", lax.rem(core, 2))
        number("other", rising != lower)
        for s in range(1, line):
            number(("hop", s), jnp.where(rising, z > s, z < line - 1 - s))
        for j in range(members):
            number(("to", j), lax.rem(member + members - j, members))
        for k in range(1, line):
            number(("send", k), lax.rem(jnp.where(lower, z - k, z + k) + line, line))
            onward = jnp.where(rising, z + line - k, z - line + k)
            number(("keep", k), jnp.clip(onward, 0, line - 1))
        source = [lax.rem(core + lo - o, lo) for o in range(lo)]
        for j in range(line):
            number(("slot", j), lax.rem(jnp.where(lower, z + j, z - j) + line, line))
            if j == 0:
                places = source
            else:
                down = fell(j)
                first = jnp.where(down == 1, 1 - group, group)
                places = [
                    jnp.where((h // nh) == down, first, 1 - first) * nh + h % nh for h in source
                ]
            for p, value in enumerate(places):
                number(("piece", j, p), value)
        ids = jnp.stack(numbers)

        kept = [None]

        def use_weight(first, n, ids):
            kept[0] = weight_slots(
                ids,
                at[("slot", first)],
                lo,
                [x for j in range(first, first + n) for x in whole[j]],
                width,
                scaled,
                out_grad,
                gate,
                up,
                in_scale,
                slot,
                kept[0],
            )

        weight_first()
        made = prepare(gate, up, in_scale, out_grad, out_scale, slot, line, nh)
        turned, scaled = list(made[:2]), list(made[2:])
        lefts, rights = [turned], [scaled]
        for o in range(1, lo):
            rights.append([to_chip(x, every, o) for x in scaled])
            lefts.append([to_chip(x, every, o) for x in turned])

        got = [None] * line

        def works(a, c, k):
            if k == 0:
                return True
            if a < line // 2:
                return (c < nh) == (k > a)
            return (c >= nh) == (k > line - 1 - a)

        def exchange(k, blocks):
            got[k] = []
            for j in range(1, members):
                pairs = [
                    (dev(a, c, (m + j) % members), dev(a, c, m))
                    for m in range(members)
                    for a in chips
                    for c in range(lo)
                    if works(a, c, k)
                ]
                got[k].append(lax.ppermute(blocks[j - 1], ("member", "fsdp"), pairs))

        others = [at[("to", j)] for j in range(1, members)]
        items = [(at[("send", 1)], j, BF16) for j in range(members - 1)]
        ids, arrived[1] = tie(ids, arrived[1])
        made = partials(ids, at, items, others, lefts, rights, members)
        behind = weight
        exchange(1, made)
        if line > 2:
            weight_next(2)
        weight_mine(1)
        whole[0] = [weight] + [to_chip(behind, every, o) for o in range(1, lo)]
        ids, whole[0] = tie(ids, whole[0])
        order = list(range(2, line)) + [0]
        items = []
        for k in order:
            row = at[("send", k)] if k else None
            items += [(row, j, BF16) for j in range(1, members)]
        for k in order:
            row = at[("keep", k)] if k else None
            items.append((row, 0, BF16 if k else F32))
        items.append((at[("keep", 1)], 0, BF16))
        made = partials(ids, at, items, [at[("to", 0)]] + others, lefts, rights, members)
        twin[1], made = tie(twin[1], made)
        to_send = {
            k: made[n * (members - 1) : (n + 1) * (members - 1)] for n, k in enumerate(order)
        }
        sums = dict(zip(order + [1], made[len(order) * (members - 1) :]))

        coming = []
        joint = shard == weight.shape[0] and columns * 2 == weight.shape[1]

        def line_sum(s):
            return hop(
                ids,
                (at["other"], at[("hop", s)]),
                sums[s],
                list(got[s]),
                list(got[line - s]) if 2 * s > line else [],
                list(coming),
                [arrived[s + 1]] if s + 2 < line and joint else [],
            )

        def line_send(s, total):
            rises, falls = list(range(s)), list(range(line - s, line))
            if s + 2 < line and joint:
                rises += range(s + 1, line - 1)
                falls += range(1, line - 1 - s)
                arrived[s + 2] = line_step(total, rises, falls)
                coming[:] = [arrived[s + 2]]
                return
            coming[:] = [line_step(total, rises, falls)]
            if s + 2 < line:
                weight_next(s + 2)

        spread(1, core)
        whole[1][0], got[1] = tie(whole[1][0], got[1])
        for s in range(1, line):
            k = s + 1 if s + 1 < line else 0
            to_send[k], got[s] = tie(to_send[k], got[s])
            total = line_sum(s)
            ids, total = tie(ids, total)
            here, total = tie(core, total)
            line_send(s, total)
            exchange(k, to_send[k])
            if s + 1 < line:
                weight_mine(s + 1)
            if s > 1:
                spread(s, here)
            first = s if s > 1 else 0
            use_weight(first, s + 1 - first, ids)
            if s + 1 < line:
                (got[k], coming[0]), kept[0] = tie((got[k], coming[0]), kept[0])
                twin[s + 1], kept[0] = tie(twin[s + 1], kept[0])
                if s + 2 < line and joint:
                    arrived[s + 2] = coming[0]
        both = jnp.concatenate(kept[0][2:], axis=1)
        if lo & (lo - 1):
            both = lax.psum(both, "fsdp")
        else:
            stage = 1
            while stage < lo:
                both = both + lax.ppermute(both, "fsdp", [(i, i ^ stage) for i in range(fsdp)])
                stage *= 2
            terms = [both] + [
                lax.ppermute(both, "fsdp", [((i + r * lo) % fsdp, i) for i in range(fsdp)])
                for r in range(1, line)
            ]
            (got[0], coming[0]), terms[1] = tie((got[0], coming[0]), terms[1])
            both = None
            for a in chips:
                term = terms[0]
                for r in range(1, line):
                    term = jnp.where(lax.rem(z + r, line) == a, terms[r], term)
                both = term if both is None else both + term
        top, bottom = coming[0][:, :columns], coming[0][:, columns:]
        landed = []
        for part in range(2):
            pairs = [(i, 2 * i + part) for i in halves]
            pairs += [(nh + i, 2 * i + 1 - part) for i in halves]
            x = jnp.where(rising, bottom, top) if part else jnp.where(rising, top, bottom)
            if any(c != d for c, d in pairs):
                x = lax.ppermute(
                    x, "fsdp", [(dev(a, c), dev(a, d)) for a in chips for c, d in pairs]
                )
            landed.append(x)
        grad_down = sums[0]
        for x in got[0] + landed:
            grad_down = grad_down + x.astype(F32)
        return kept[0][0], kept[0][1], grad_down, both[:, :ff], both[:, ff:]

    return run


def solution(mesh):
    rows = P(("groups", "member", "fsdp"), None)
    in_specs = (
        rows,
        rows,
        rows,
        P("member", None),
        P("member", None),
        P("fsdp", None),
        P(("groups", "member", "fsdp")),
    )
    out_specs = (
        rows,
        rows,
        P(("groups", "fsdp"), "member"),
        P(("groups", "member"), None),
        P(("groups", "member"), None),
    )
    run = on_device(mesh.shape["groups"], mesh.shape["member"], mesh.shape["fsdp"])
    return jax.shard_map(run, mesh=mesh, in_specs=in_specs, out_specs=out_specs, check_vma=False)
```

```python
import functools
import math

import jax
import jax.numpy as jnp
from jax import lax
from jax.experimental import pallas as pl
from jax.experimental.pallas import tpu as pltpu
from jax.sharding import PartitionSpec as P

F32 = jnp.float32
BF16 = jnp.bfloat16
VMEM_BYTES = 60 * 1024 * 1024
ROOT_2_PI = math.sqrt(2.0 / math.pi)
CUBIC = 0.044715
SHORT = pl.CostEstimate(flops=1, bytes_accessed=1, transcendentals=0)


def tanh_of(x):
    return jnp.tanh(ROOT_2_PI * (x + CUBIC * (x * x * x)))


def pick_rows(slot, scale):
    rows = jnp.zeros((slot.shape[0], scale.shape[1]), F32)
    for k in range(scale.shape[0]):
        rows = jnp.where(slot == k, scale[k : k + 1, :], rows)
    return rows


def prepare_kernel(nh, gate_ref, up_ref, in_scale_ref, grad_ref, out_scale_ref, slot_ref, *outs):
    slot = slot_ref[...]
    gate = gate_ref[...].astype(F32)
    gelu = gate * (0.5 * (1.0 + tanh_of(gate)))
    act = gelu * up_ref[...].astype(F32)
    turned = (act * pick_rows(slot, in_scale_ref[...])).T.astype(BF16)
    shard = outs[0].shape[1] // nh
    for i in range(nh):
        for p in range(2):
            first = (2 * i + p) * shard
            outs[p][0, i * shard : (i + 1) * shard, :] = turned[first : first + shard]
    scaled = (grad_ref[...].astype(F32) * pick_rows(slot, out_scale_ref[...])).astype(BF16)
    half = scaled.shape[0] // 2
    outs[2][...] = scaled[:half]
    outs[3][...] = scaled[half:]


def prepare(gate, up, in_scale, out_grad, out_scale, slot, blocks, nh):
    tokens, ff = gate.shape
    d = out_grad.shape[1]
    width, columns = ff // blocks, d // blocks
    mem = in_scale.shape[0]
    spec = lambda shape: pl.BlockSpec(shape, lambda i: (0, i))
    turned = jax.ShapeDtypeStruct((blocks, width // 2, tokens), BF16)
    scaled = jax.ShapeDtypeStruct((tokens // 2, d), BF16)
    return pl.pallas_call(
        functools.partial(prepare_kernel, nh),
        out_shape=[turned, turned, scaled, scaled],
        grid=(blocks,),
        in_specs=[
            spec((tokens, width)),
            spec((tokens, width)),
            spec((mem, width)),
            spec((tokens, columns)),
            spec((mem, columns)),
            pl.BlockSpec((tokens, 1), lambda i: (0, 0)),
        ],
        out_specs=[pl.BlockSpec((1, width // 2, tokens), lambda i: (i, 0, 0))] * 2
        + [spec((tokens // 2, columns))] * 2,
        compiler_params=pltpu.CompilerParams(vmem_limit_bytes=VMEM_BYTES),
        cost_estimate=SHORT,
    )(gate, up, in_scale, out_grad, out_scale, slot)


def partials_kernel(lo, items, n_columns, own_at, ids_ref, *refs):
    lefts, refs = [refs[2 * i : 2 * i + 2] for i in range(lo)], refs[2 * lo :]
    if own_at is not None:
        owns, refs = [refs[2 * i : 2 * i + 2] for i in range(lo)], refs[2 * lo :]
    rights = []
    for _ in range(n_columns):
        rights.append(jnp.concatenate([r[...] for r in refs[: 2 * lo]], axis=0))
        refs = refs[2 * lo :]
    single = lefts[0][0].shape[0] == 1
    for (row, column, _), out in zip(items, refs):
        if row is None:
            odd = ids_ref[own_at] == 1
            left = jnp.concatenate([jnp.where(odd, b[0], a[0]) for a, b in owns], axis=1)
            total = jnp.dot(left, rights[column], preferred_element_type=F32)
            out[...] = total.astype(out.dtype)
            continue
        block = 0 if single else ids_ref[row]
        shard = lefts[0][0].shape[1]
        for p in range(2):
            left = jnp.concatenate([pair[p][block] for pair in lefts], axis=1)
            total = jnp.dot(left, rights[column], preferred_element_type=F32)
            out[p * shard : (p + 1) * shard, :] = total.astype(out.dtype)


def partials(ids, at, items, column_at, lefts, rights, members):
    lo = len(lefts)
    line, part, tokens = lefts[0][0].shape
    shard = part // (lo // 2)
    width = rights[0][0].shape[1] // members
    single = len({row for row, _, _ in items}) == 1
    tile = max(width // (2 if single else 4), 128)
    tiles = width // tile
    if single:
        row = items[0][0]
        left_spec = pl.BlockSpec((1, shard, tokens), lambda i, ids: (ids[row], ids[at["half"]], 0))
    else:
        left_spec = pl.BlockSpec((line, shard, tokens), lambda i, ids: (0, ids[at["half"]], 0))
    flat = [x for pair in lefts for x in pair]
    ins, specs = list(flat), [left_spec] * len(flat)
    own_at = None
    if any(row is None for row, _, _ in items):
        own_at = at["odd"]
        ins += flat
        specs += [
            pl.BlockSpec((1, shard, tokens), lambda i, ids: (ids[at["z"]], ids[at["own"]], 0))
        ] * len(flat)
    for where in column_at:
        ins += [x for pair in rights for x in pair]
        specs += [
            pl.BlockSpec((tokens // 2, tile), lambda i, ids, w=where: (0, ids[w] * tiles + i))
        ] * (2 * lo)
    shapes = [
        jax.ShapeDtypeStruct((shard if row is None else 2 * shard, width), dtype)
        for row, _, dtype in items
    ]
    return pl.pallas_call(
        functools.partial(partials_kernel, lo, items, len(column_at), own_at),
        out_shape=shapes,
        grid_spec=pltpu.PrefetchScalarGridSpec(
            num_scalar_prefetch=1,
            grid=(tiles,),
            in_specs=specs,
            out_specs=[pl.BlockSpec((s.shape[0], tile), lambda i, ids: (0, i)) for s in shapes],
        ),
        compiler_params=pltpu.CompilerParams(vmem_limit_bytes=VMEM_BYTES),
        cost_estimate=SHORT,
    )(ids, *ins)


def hop_kernel(n_got, either, n_coming, flags, ids_ref, sum_ref, *refs):
    gots, refs = refs[: n_got * (1 + either)], refs[n_got * (1 + either) :]
    out_ref = refs[-1]
    total = sum_ref[...].astype(F32)
    for i in range(n_got):
        one = gots[i][...].astype(F32)
        if either:
            one = jnp.where(ids_ref[flags[0]] == 1, gots[n_got + i][...].astype(F32), one)
        total = total + one
    for i in range(n_coming):
        total = total + refs[i][...].astype(F32)
    if len(refs) > n_coming + 1:
        total = jnp.where(ids_ref[flags[1]] == 1, refs[n_coming][...].astype(F32), total)
    out_ref[...] = total.astype(BF16)


def hop(ids, flags, own, got, other, coming, weight):
    rows, columns = own.shape
    stacked = pl.BlockSpec((rows // 2, columns), lambda i, ids: (i, 0))
    beside = pl.BlockSpec((rows // 2, columns), lambda i, ids: (0, i))
    ins = [own] + got + other + coming + weight
    return pl.pallas_call(
        functools.partial(hop_kernel, len(got), bool(other), len(coming), flags),
        out_shape=jax.ShapeDtypeStruct((rows // 2, 2 * columns), BF16),
        grid_spec=pltpu.PrefetchScalarGridSpec(
            num_scalar_prefetch=1,
            grid=(2,),
            in_specs=[stacked] * (1 + len(got) + len(other))
            + [beside] * (len(coming) + len(weight)),
            out_specs=beside,
        ),
        compiler_params=pltpu.CompilerParams(vmem_limit_bytes=VMEM_BYTES),
        cost_estimate=SHORT,
    )(ids, *ins)


def slot_kernel(n, lo, kept, base, ids_ref, *refs):
    pieces, refs = refs[: n * lo], refs[n * lo :]
    scaled_refs, refs = refs[:2], refs[2:]
    out_grad_ref, gate_ref, up_ref, in_scale_ref, slot_ref = refs[:5]
    refs = refs[5:]
    if kept:
        before_ref, refs = refs[3], refs[4:]
    grad_gate_ref, grad_up_ref, sum_in_ref, sum_out_ref, weight_ref, sems = refs
    shard = pieces[0].shape[0]

    step = pl.program_id(0)

    def copy_of(i, p):
        start = pl.multiple_of(ids_ref[base + i * (lo + 1) + 1 + p] * shard, shard)
        return pltpu.make_async_copy(
            pieces[i * lo + p], weight_ref.at[i, pl.ds(start, shard)], sems.at[i, p]
        )

    @pl.when(step == 0)
    def _():
        for i in range(n):
            for p in range(lo):
                copy_of(i, p).start()

    slot = slot_ref[...]
    gate = gate_ref[...].astype(F32)
    up = up_ref[...].astype(F32)
    tanh = tanh_of(gate)
    cdf = 0.5 * (1.0 + tanh)
    slope = cdf + gate * (0.5 * ROOT_2_PI) * (1.0 - tanh * tanh) * (
        1.0 + (3.0 * CUBIC) * (gate * gate)
    )
    gelu = gate * cdf
    act = gelu * up
    row_in = pick_rows(slot, in_scale_ref[...])
    hidden = (act * row_in).astype(BF16)

    for i in range(n):

        @pl.when(step == i)
        def _():
            for p in range(lo):
                copy_of(i, p).wait()

    weight = weight_ref[step]
    scaled = jnp.concatenate([r[...] for r in scaled_refs], axis=0)
    grad_hidden = lax.dot_general(
        scaled, weight, (((1,), (1,)), ((), ())), preferred_element_type=F32
    )
    grad_act = grad_hidden * row_in
    grad_gate_ref[...] = (grad_act * up * slope).astype(BF16)
    grad_up_ref[...] = (grad_act * gelu).astype(BF16)
    product = grad_hidden * act
    forward = jnp.dot(hidden, weight, preferred_element_type=F32)
    forward = forward * out_grad_ref[...].astype(F32)
    mores = []
    for k in range(in_scale_ref.shape[0]):
        mine = slot == k
        row = slice(k, k + 1)
        sum_in_ref[row, :] = jnp.sum(jnp.where(mine, product, 0.0), axis=0, keepdims=True)
        more = jnp.sum(jnp.where(mine, forward, 0.0), axis=0, keepdims=True)
        mores.append(more)

    @pl.when(step == 0)
    def _():
        for k, more in enumerate(mores):
            row = slice(k, k + 1)
            sum_out_ref[row, :] = before_ref[row, :] + more if kept else more

    @pl.when(step > 0)
    def _():
        for k, more in enumerate(mores):
            row = slice(k, k + 1)
            sum_out_ref[row, :] = sum_out_ref[row, :] + more


def weight_slots(ids, base, lo, pieces, width, scaled, out_grad, gate, up, in_scale, slot, kept):
    tokens, ff = gate.shape
    d = out_grad.shape[1]
    mem = in_scale.shape[0]
    n = len(pieces) // lo
    column = lambda rows: pl.BlockSpec(
        (rows, width), lambda i, ids: (0, ids[base + i * (lo + 1)])
    )
    full = lambda shape: pl.BlockSpec(shape, lambda i, ids: (0, 0))
    anywhere = pl.BlockSpec(memory_space=pl.ANY)
    ins = list(pieces) + list(scaled) + [out_grad, gate, up, in_scale, slot]
    specs = [anywhere] * len(pieces) + [full((tokens // 2, d))] * 2
    specs += [full((tokens, d)), column(tokens), column(tokens), column(mem), full((tokens, 1))]
    aliases = {}
    if kept is not None:
        aliases = {1 + len(ins) + i: i for i in range(3)}
        ins += list(kept)
        specs += [anywhere] * 3 + [full((mem, d))]
    return pl.pallas_call(
        functools.partial(slot_kernel, n, lo, kept is not None, base),
        out_shape=[
            jax.ShapeDtypeStruct((tokens, ff), BF16),
            jax.ShapeDtypeStruct((tokens, ff), BF16),
            jax.ShapeDtypeStruct((mem, ff), F32),
            jax.ShapeDtypeStruct((mem, d), F32),
        ],
        grid_spec=pltpu.PrefetchScalarGridSpec(
            num_scalar_prefetch=1,
            grid=(n,),
            in_specs=specs,
            out_specs=[column(tokens), column(tokens), column(mem), full((mem, d))],
            scratch_shapes=[
                pltpu.VMEM((n, width, d), BF16),
                pltpu.SemaphoreType.DMA((n, lo)),
            ],
        ),
        input_output_aliases=aliases,
        compiler_params=pltpu.CompilerParams(vmem_limit_bytes=VMEM_BYTES),
        cost_estimate=SHORT,
    )(ids, *ins)


def on_device(groups, members, fsdp):
    def run(gate, up, out_grad, in_scale, out_scale, weight, member_slot):
        tokens, ff = gate.shape
        shard = weight.shape[0]
        columns = out_grad.shape[1] // members
        lo = max(128 // math.gcd(shard, 128), 2)
        line, nh = fsdp // lo, lo // 2
        assert groups == 2 and line * lo == fsdp and line > 1
        width = lo * shard
        group = lax.axis_index("groups")
        member = lax.axis_index("member")
        place_id = lax.axis_index("fsdp")
        z, core = place_id // lo, lax.rem(place_id, lo)
        lower, rising = z < line // 2, core < nh
        slot = member_slot[:, None]
        chips = range(line)
        halves = range(nh)

        def tie(x, y):
            return lax.optimization_barrier((x, y))

        def dev(zz, c, outer=0):
            return (outer * line + zz) * lo + c

        def line_step(x, rises, falls):
            pairs = [(dev(a, i), dev(a + 1, i)) for a in rises for i in halves]
            pairs += [(dev(a, nh + i), dev(a - 1, nh + i)) for a in falls for i in halves]
            return lax.ppermute(x, "fsdp", pairs)

        def to_chip(x, sources, o):
            return lax.ppermute(
                x, "fsdp", [(dev(a, c), dev(a, (c + o) % lo)) for a in chips for c in sources(a)]
            )

        every = lambda a: range(lo)

        arrived, mine, twin = [None] * line, [None] * line, [None] * line
        whole = [None] * line

        def weight_first():
            pairs = []
            for g in range(2):
                for a in chips:
                    for i in halves:
                        if a + 1 < line:
                            pairs.append((dev(a, g * nh + i, g), dev(a + 1, i, g)))
                        if a > 0:
                            pairs.append((dev(a, (1 - g) * nh + i, g), dev(a - 1, nh + i, g)))
            arrived[1] = lax.ppermute(weight, ("groups", "fsdp"), pairs)

        def weight_next(s):
            arrived[s] = line_step(
                arrived[s - 1], range(s - 1, line - 1), range(1, line - s + 1)
            )

        def falls(a, j):
            return a + j < line if a < line // 2 else a < j

        def fell(j):
            table = [int(falls(a, j)) for a in chips]
            flag = jnp.int32(table[-1])
            for a in range(line - 1):
                flag = jnp.where(z == a, table[a], flag)
            return flag

        def holders(j):
            return lambda a: [nh * falls(a, j) + i for i in halves]

        def weight_mine(j):
            block = arrived[j]
            if 2 * j > line:
                straight = jnp.where(lower, z + j < line, z >= j)
                block = jnp.where(straight, block, arrived[line - j])
            mine[j] = block
            pairs = [
                (dev(a, h, g), dev(a, (h + nh) % lo, 1 - g))
                for g in range(2)
                for a in chips
                for h in holders(j)(a)
            ]
            twin[j] = lax.ppermute(block, ("groups", "fsdp"), pairs)

        def spread(j, core):
            held = jnp.where((core >= nh) == (fell(j) == 1), mine[j], twin[j])
            whole[j] = [held] + [to_chip(held, every, o) for o in range(1, lo)]

        numbers, at = [], {}

        def number(name, value):
            at[name] = len(numbers)
            numbers.append(jnp.asarray(value, jnp.int32))

        number("z", z)
        number("half", lax.rem(core, nh) if nh > 1 else 0)
        number("own", core // 2)
        number("odd", lax.rem(core, 2))
        number("other", rising != lower)
        for s in range(1, line):
            number(("hop", s), jnp.where(rising, z > s, z < line - 1 - s))
        for j in range(members):
            number(("to", j), lax.rem(member + members - j, members))
        for k in range(1, line):
            number(("send", k), lax.rem(jnp.where(lower, z - k, z + k) + line, line))
            onward = jnp.where(rising, z + line - k, z - line + k)
            number(("keep", k), jnp.clip(onward, 0, line - 1))
        source = [lax.rem(core + lo - o, lo) for o in range(lo)]
        for j in range(line):
            number(("slot", j), lax.rem(jnp.where(lower, z + j, z - j) + line, line))
            if j == 0:
                places = source
            else:
                down = fell(j)
                first = jnp.where(down == 1, 1 - group, group)
                places = [
                    jnp.where((h // nh) == down, first, 1 - first) * nh + h % nh for h in source
                ]
            for p, value in enumerate(places):
                number(("piece", j, p), value)
        ids = jnp.stack(numbers)

        kept = [None]

        def use_weight(first, n, ids):
            kept[0] = weight_slots(
                ids,
                at[("slot", first)],
                lo,
                [x for j in range(first, first + n) for x in whole[j]],
                width,
                scaled,
                out_grad,
                gate,
                up,
                in_scale,
                slot,
                kept[0],
            )

        weight_first()
        made = prepare(gate, up, in_scale, out_grad, out_scale, slot, line, nh)
        turned, scaled = list(made[:2]), list(made[2:])
        lefts, rights = [turned], [scaled]
        for o in range(1, lo):
            rights.append([to_chip(x, every, o) for x in scaled])
            lefts.append([to_chip(x, every, o) for x in turned])

        got = [None] * line

        def works(a, c, k):
            if k == 0:
                return True
            if a < line // 2:
                return (c < nh) == (k > a)
            return (c >= nh) == (k > line - 1 - a)

        def exchange(k, blocks):
            got[k] = []
            for j in range(1, members):
                pairs = [
                    (dev(a, c, (m + j) % members), dev(a, c, m))
                    for m in range(members)
                    for a in chips
                    for c in range(lo)
                    if works(a, c, k)
                ]
                got[k].append(lax.ppermute(blocks[j - 1], ("member", "fsdp"), pairs))

        others = [at[("to", j)] for j in range(1, members)]
        items = [(at[("send", 1)], j, BF16) for j in range(members - 1)]
        ids, arrived[1] = tie(ids, arrived[1])
        made = partials(ids, at, items, others, lefts, rights, members)
        behind = weight
        exchange(1, made)
        if line > 2:
            weight_next(2)
        weight_mine(1)
        whole[0] = [weight] + [to_chip(behind, every, o) for o in range(1, lo)]
        ids, whole[0] = tie(ids, whole[0])
        order = list(range(2, line)) + [0]
        items = []
        for k in order:
            row = at[("send", k)] if k else None
            items += [(row, j, BF16) for j in range(1, members)]
        for k in order:
            row = at[("keep", k)] if k else None
            items.append((row, 0, BF16 if k else F32))
        items.append((at[("keep", 1)], 0, BF16))
        made = partials(ids, at, items, [at[("to", 0)]] + others, lefts, rights, members)
        twin[1], made = tie(twin[1], made)
        to_send = {
            k: made[n * (members - 1) : (n + 1) * (members - 1)] for n, k in enumerate(order)
        }
        sums = dict(zip(order + [1], made[len(order) * (members - 1) :]))

        coming = []
        joint = shard == weight.shape[0] and columns * 2 == weight.shape[1]

        def line_sum(s):
            return hop(
                ids,
                (at["other"], at[("hop", s)]),
                sums[s],
                list(got[s]),
                list(got[line - s]) if 2 * s > line else [],
                list(coming),
                [arrived[s + 1]] if s + 2 < line and joint else [],
            )

        def line_send(s, total):
            rises, falls = list(range(s)), list(range(line - s, line))
            if s + 2 < line and joint:
                rises += range(s + 1, line - 1)
                falls += range(1, line - 1 - s)
                arrived[s + 2] = line_step(total, rises, falls)
                coming[:] = [arrived[s + 2]]
                return
            coming[:] = [line_step(total, rises, falls)]
            if s + 2 < line:
                weight_next(s + 2)

        spread(1, core)
        whole[1][0], got[1] = tie(whole[1][0], got[1])
        for s in range(1, line):
            k = s + 1 if s + 1 < line else 0
            to_send[k], got[s] = tie(to_send[k], got[s])
            total = line_sum(s)
            ids, total = tie(ids, total)
            here, total = tie(core, total)
            line_send(s, total)
            exchange(k, to_send[k])
            if s + 1 < line:
                weight_mine(s + 1)
            if s > 1:
                spread(s, here)
            first = s if s > 1 else 0
            use_weight(first, s + 1 - first, ids)
            if s + 1 < line:
                (got[k], coming[0]), kept[0] = tie((got[k], coming[0]), kept[0])
                twin[s + 1], kept[0] = tie(twin[s + 1], kept[0])
                if s + 2 < line and joint:
                    arrived[s + 2] = coming[0]
        both = jnp.concatenate(kept[0][2:], axis=1)
        if lo & (lo - 1):
            both = lax.psum(both, "fsdp")
        else:
            stage = 1
            while stage < lo:
                both = both + lax.ppermute(both, "fsdp", [(i, i ^ stage) for i in range(fsdp)])
                stage *= 2
            terms = [both] + [
                lax.ppermute(both, "fsdp", [((i + r * lo) % fsdp, i) for i in range(fsdp)])
                for r in range(1, line)
            ]
            (got[0], coming[0]), terms[1] = tie((got[0], coming[0]), terms[1])
            both = None
            for a in chips:
                term = terms[0]
                for r in range(1, line):
                    term = jnp.where(lax.rem(z + r, line) == a, terms[r], term)
                both = term if both is None else both + term
        top, bottom = coming[0][:, :columns], coming[0][:, columns:]
        landed = []
        for part in range(2):
            pairs = [(i, 2 * i + part) for i in halves]
            pairs += [(nh + i, 2 * i + 1 - part) for i in halves]
            x = jnp.where(rising, bottom, top) if part else jnp.where(rising, top, bottom)
            if any(c != d for c, d in pairs):
                x = lax.ppermute(
                    x, "fsdp", [(dev(a, c), dev(a, d)) for a in chips for c, d in pairs]
                )
            landed.append(x)
        grad_down = sums[0]
        for x in got[0] + landed:
            grad_down = grad_down + x.astype(F32)
        return kept[0][0], kept[0][1], grad_down, both[:, :ff], both[:, ff:]

    return run


def solution(mesh):
    rows = P(("groups", "member", "fsdp"), None)
    in_specs = (
        rows,
        rows,
        rows,
        P("member", None),
        P("member", None),
        P("fsdp", None),
        P(("groups", "member", "fsdp")),
    )
    out_specs = (
        rows,
        rows,
        P(("groups", "fsdp"), "member"),
        P(("groups", "member"), None),
        P(("groups", "member"), None),
    )
    run = on_device(mesh.shape["groups"], mesh.shape["member"], mesh.shape["fsdp"])
    return jax.shard_map(run, mesh=mesh, in_specs=in_specs, out_specs=out_specs, check_vma=False)
```

```python
import functools
import math

import jax
import jax.numpy as jnp
from jax import lax
from jax.experimental import pallas as pl
from jax.experimental.pallas import tpu as pltpu
from jax.sharding import PartitionSpec as P

F32 = jnp.float32
BF16 = jnp.bfloat16
VMEM_BYTES = 60 * 1024 * 1024
ROOT_2_PI = math.sqrt(2.0 / math.pi)
CUBIC = 0.044715
SHORT = pl.CostEstimate(flops=1, bytes_accessed=1, transcendentals=0)


def tanh_of(x):
    return jnp.tanh(ROOT_2_PI * (x + CUBIC * (x * x * x)))


def pick_rows(slot, scale):
    rows = jnp.zeros((slot.shape[0], scale.shape[1]), F32)
    for k in range(scale.shape[0]):
        rows = jnp.where(slot == k, scale[k : k + 1, :], rows)
    return rows


def prepare_kernel(nh, gate_ref, up_ref, in_scale_ref, grad_ref, out_scale_ref, slot_ref, *outs):
    slot = slot_ref[...]
    gate = gate_ref[...].astype(F32)
    gelu = gate * (0.5 * (1.0 + tanh_of(gate)))
    act = gelu * up_ref[...].astype(F32)
    turned = (act * pick_rows(slot, in_scale_ref[...])).T.astype(BF16)
    shard = outs[0].shape[1] // nh
    for i in range(nh):
        for p in range(2):
            first = (2 * i + p) * shard
            outs[p][0, i * shard : (i + 1) * shard, :] = turned[first : first + shard]
    scaled = (grad_ref[...].astype(F32) * pick_rows(slot, out_scale_ref[...])).astype(BF16)
    half = scaled.shape[0] // 2
    outs[2][...] = scaled[:half]
    outs[3][...] = scaled[half:]


def prepare(gate, up, in_scale, out_grad, out_scale, slot, blocks, nh):
    tokens, ff = gate.shape
    d = out_grad.shape[1]
    width, columns = ff // blocks, d // blocks
    mem = in_scale.shape[0]
    spec = lambda shape: pl.BlockSpec(shape, lambda i: (0, i))
    turned = jax.ShapeDtypeStruct((blocks, width // 2, tokens), BF16)
    scaled = jax.ShapeDtypeStruct((tokens // 2, d), BF16)
    return pl.pallas_call(
        functools.partial(prepare_kernel, nh),
        out_shape=[turned, turned, scaled, scaled],
        grid=(blocks,),
        in_specs=[
            spec((tokens, width)),
            spec((tokens, width)),
            spec((mem, width)),
            spec((tokens, columns)),
            spec((mem, columns)),
            pl.BlockSpec((tokens, 1), lambda i: (0, 0)),
        ],
        out_specs=[pl.BlockSpec((1, width // 2, tokens), lambda i: (i, 0, 0))] * 2
        + [spec((tokens // 2, columns))] * 2,
        compiler_params=pltpu.CompilerParams(vmem_limit_bytes=VMEM_BYTES),
        cost_estimate=SHORT,
    )(gate, up, in_scale, out_grad, out_scale, slot)


def partials_kernel(lo, items, n_columns, own_at, ids_ref, *refs):
    lefts, refs = [refs[2 * i : 2 * i + 2] for i in range(lo)], refs[2 * lo :]
    if own_at is not None:
        owns, refs = [refs[2 * i : 2 * i + 2] for i in range(lo)], refs[2 * lo :]
    rights = []
    for _ in range(n_columns):
        rights.append(jnp.concatenate([r[...] for r in refs[: 2 * lo]], axis=0))
        refs = refs[2 * lo :]
    single = lefts[0][0].shape[0] == 1
    for (row, column, _), out in zip(items, refs):
        if row is None:
            odd = ids_ref[own_at] == 1
            left = jnp.concatenate([jnp.where(odd, b[0], a[0]) for a, b in owns], axis=1)
            total = jnp.dot(left, rights[column], preferred_element_type=F32)
            out[...] = total.astype(out.dtype)
            continue
        block = 0 if single else ids_ref[row]
        shard = lefts[0][0].shape[1]
        for p in range(2):
            left = jnp.concatenate([pair[p][block] for pair in lefts], axis=1)
            total = jnp.dot(left, rights[column], preferred_element_type=F32)
            out[p * shard : (p + 1) * shard, :] = total.astype(out.dtype)


def partials(ids, at, items, column_at, lefts, rights, members):
    lo = len(lefts)
    line, part, tokens = lefts[0][0].shape
    shard = part // (lo // 2)
    width = rights[0][0].shape[1] // members
    single = len({row for row, _, _ in items}) == 1
    tile = max(width // (2 if single else 4), 128)
    tiles = width // tile
    if single:
        row = items[0][0]
        left_spec = pl.BlockSpec((1, shard, tokens), lambda i, ids: (ids[row], ids[at["half"]], 0))
    else:
        left_spec = pl.BlockSpec((line, shard, tokens), lambda i, ids: (0, ids[at["half"]], 0))
    flat = [x for pair in lefts for x in pair]
    ins, specs = list(flat), [left_spec] * len(flat)
    own_at = None
    if any(row is None for row, _, _ in items):
        own_at = at["odd"]
        ins += flat
        specs += [
            pl.BlockSpec((1, shard, tokens), lambda i, ids: (ids[at["z"]], ids[at["own"]], 0))
        ] * len(flat)
    for where in column_at:
        ins += [x for pair in rights for x in pair]
        specs += [
            pl.BlockSpec((tokens // 2, tile), lambda i, ids, w=where: (0, ids[w] * tiles + i))
        ] * (2 * lo)
    shapes = [
        jax.ShapeDtypeStruct((shard if row is None else 2 * shard, width), dtype)
        for row, _, dtype in items
    ]
    return pl.pallas_call(
        functools.partial(partials_kernel, lo, items, len(column_at), own_at),
        out_shape=shapes,
        grid_spec=pltpu.PrefetchScalarGridSpec(
            num_scalar_prefetch=1,
            grid=(tiles,),
            in_specs=specs,
            out_specs=[pl.BlockSpec((s.shape[0], tile), lambda i, ids: (0, i)) for s in shapes],
        ),
        compiler_params=pltpu.CompilerParams(vmem_limit_bytes=VMEM_BYTES),
        cost_estimate=SHORT,
    )(ids, *ins)


def hop_kernel(n_got, either, n_coming, flags, ids_ref, sum_ref, *refs):
    gots, refs = refs[: n_got * (1 + either)], refs[n_got * (1 + either) :]
    out_ref = refs[-1]
    total = sum_ref[...].astype(F32)
    for i in range(n_got):
        one = gots[i][...].astype(F32)
        if either:
            one = jnp.where(ids_ref[flags[0]] == 1, gots[n_got + i][...].astype(F32), one)
        total = total + one
    for i in range(n_coming):
        total = total + refs[i][...].astype(F32)
    if len(refs) > n_coming + 1:
        total = jnp.where(ids_ref[flags[1]] == 1, refs[n_coming][...].astype(F32), total)
    out_ref[...] = total.astype(BF16)


def hop(ids, flags, own, got, other, coming, weight):
    rows, columns = own.shape
    stacked = pl.BlockSpec((rows // 4, columns), lambda i, h, ids: (2 * i + h, 0))
    beside = pl.BlockSpec((rows // 4, columns), lambda i, h, ids: (h, i))
    ins = [own] + got + other + coming + weight
    return pl.pallas_call(
        functools.partial(hop_kernel, len(got), bool(other), len(coming), flags),
        out_shape=jax.ShapeDtypeStruct((rows // 2, 2 * columns), BF16),
        grid_spec=pltpu.PrefetchScalarGridSpec(
            num_scalar_prefetch=1,
            grid=(2, 2),
            in_specs=[stacked] * (1 + len(got) + len(other))
            + [beside] * (len(coming) + len(weight)),
            out_specs=beside,
        ),
        compiler_params=pltpu.CompilerParams(vmem_limit_bytes=VMEM_BYTES),
        cost_estimate=SHORT,
    )(ids, *ins)


def slot_kernel(n, lo, kept, base, ids_ref, *refs):
    pieces, refs = refs[: n * lo], refs[n * lo :]
    scaled_refs, refs = refs[:2], refs[2:]
    out_grad_ref, gate_ref, up_ref, in_scale_ref, slot_ref = refs[:5]
    refs = refs[5:]
    if kept:
        before_ref, refs = refs[3], refs[4:]
    grad_gate_ref, grad_up_ref, sum_in_ref, sum_out_ref, weight_ref, sems = refs
    shard = pieces[0].shape[0]

    step = pl.program_id(0)

    def copy_of(i, p):
        start = pl.multiple_of(ids_ref[base + i * (lo + 1) + 1 + p] * shard, shard)
        return pltpu.make_async_copy(
            pieces[i * lo + p], weight_ref.at[i, pl.ds(start, shard)], sems.at[i, p]
        )

    @pl.when(step == 0)
    def _():
        for i in range(n):
            for p in range(lo):
                copy_of(i, p).start()

    slot = slot_ref[...]
    gate = gate_ref[...].astype(F32)
    up = up_ref[...].astype(F32)
    tanh = tanh_of(gate)
    cdf = 0.5 * (1.0 + tanh)
    slope = cdf + gate * (0.5 * ROOT_2_PI) * (1.0 - tanh * tanh) * (
        1.0 + (3.0 * CUBIC) * (gate * gate)
    )
    gelu = gate * cdf
    act = gelu * up
    row_in = pick_rows(slot, in_scale_ref[...])
    hidden = (act * row_in).astype(BF16)

    for i in range(n):

        @pl.when(step == i)
        def _():
            for p in range(lo):
                copy_of(i, p).wait()

    weight = weight_ref[step]
    scaled = jnp.concatenate([r[...] for r in scaled_refs], axis=0)
    grad_hidden = lax.dot_general(
        scaled, weight, (((1,), (1,)), ((), ())), preferred_element_type=F32
    )
    grad_act = grad_hidden * row_in
    grad_gate_ref[...] = (grad_act * up * slope).astype(BF16)
    grad_up_ref[...] = (grad_act * gelu).astype(BF16)
    product = grad_hidden * act
    forward = jnp.dot(hidden, weight, preferred_element_type=F32)
    forward = forward * out_grad_ref[...].astype(F32)
    mores = []
    for k in range(in_scale_ref.shape[0]):
        mine = slot == k
        row = slice(k, k + 1)
        sum_in_ref[row, :] = jnp.sum(jnp.where(mine, product, 0.0), axis=0, keepdims=True)
        more = jnp.sum(jnp.where(mine, forward, 0.0), axis=0, keepdims=True)
        mores.append(more)

    @pl.when(step == 0)
    def _():
        for k, more in enumerate(mores):
            row = slice(k, k + 1)
            sum_out_ref[row, :] = before_ref[row, :] + more if kept else more

    @pl.when(step > 0)
    def _():
        for k, more in enumerate(mores):
            row = slice(k, k + 1)
            sum_out_ref[row, :] = sum_out_ref[row, :] + more


def weight_slots(ids, base, lo, pieces, width, scaled, out_grad, gate, up, in_scale, slot, kept):
    tokens, ff = gate.shape
    d = out_grad.shape[1]
    mem = in_scale.shape[0]
    n = len(pieces) // lo
    column = lambda rows: pl.BlockSpec(
        (rows, width), lambda i, ids: (0, ids[base + i * (lo + 1)])
    )
    full = lambda shape: pl.BlockSpec(shape, lambda i, ids: (0, 0))
    anywhere = pl.BlockSpec(memory_space=pl.ANY)
    ins = list(pieces) + list(scaled) + [out_grad, gate, up, in_scale, slot]
    specs = [anywhere] * len(pieces) + [full((tokens // 2, d))] * 2
    specs += [full((tokens, d)), column(tokens), column(tokens), column(mem), full((tokens, 1))]
    aliases = {}
    if kept is not None:
        aliases = {1 + len(ins) + i: i for i in range(3)}
        ins += list(kept)
        specs += [anywhere] * 3 + [full((mem, d))]
    return pl.pallas_call(
        functools.partial(slot_kernel, n, lo, kept is not None, base),
        out_shape=[
            jax.ShapeDtypeStruct((tokens, ff), BF16),
            jax.ShapeDtypeStruct((tokens, ff), BF16),
            jax.ShapeDtypeStruct((mem, ff), F32),
            jax.ShapeDtypeStruct((mem, d), F32),
        ],
        grid_spec=pltpu.PrefetchScalarGridSpec(
            num_scalar_prefetch=1,
            grid=(n,),
            in_specs=specs,
            out_specs=[column(tokens), column(tokens), column(mem), full((mem, d))],
            scratch_shapes=[
                pltpu.VMEM((n, width, d), BF16),
                pltpu.SemaphoreType.DMA((n, lo)),
            ],
        ),
        input_output_aliases=aliases,
        compiler_params=pltpu.CompilerParams(vmem_limit_bytes=VMEM_BYTES),
        cost_estimate=SHORT,
    )(ids, *ins)


def on_device(groups, members, fsdp):
    def run(gate, up, out_grad, in_scale, out_scale, weight, member_slot):
        tokens, ff = gate.shape
        shard = weight.shape[0]
        columns = out_grad.shape[1] // members
        lo = max(128 // math.gcd(shard, 128), 2)
        line, nh = fsdp // lo, lo // 2
        assert groups == 2 and line * lo == fsdp and line > 1
        width = lo * shard
        group = lax.axis_index("groups")
        member = lax.axis_index("member")
        place_id = lax.axis_index("fsdp")
        z, core = place_id // lo, lax.rem(place_id, lo)
        lower, rising = z < line // 2, core < nh
        slot = member_slot[:, None]
        chips = range(line)
        halves = range(nh)

        def tie(x, y):
            return lax.optimization_barrier((x, y))

        def dev(zz, c, outer=0):
            return (outer * line + zz) * lo + c

        def line_step(x, rises, falls):
            pairs = [(dev(a, i), dev(a + 1, i)) for a in rises for i in halves]
            pairs += [(dev(a, nh + i), dev(a - 1, nh + i)) for a in falls for i in halves]
            return lax.ppermute(x, "fsdp", pairs)

        def to_chip(x, sources, o):
            return lax.ppermute(
                x, "fsdp", [(dev(a, c), dev(a, (c + o) % lo)) for a in chips for c in sources(a)]
            )

        every = lambda a: range(lo)

        arrived, mine, twin = [None] * line, [None] * line, [None] * line
        whole = [None] * line

        def weight_first():
            pairs = []
            for g in range(2):
                for a in chips:
                    for i in halves:
                        if a + 1 < line:
                            pairs.append((dev(a, g * nh + i, g), dev(a + 1, i, g)))
                        if a > 0:
                            pairs.append((dev(a, (1 - g) * nh + i, g), dev(a - 1, nh + i, g)))
            arrived[1] = lax.ppermute(weight, ("groups", "fsdp"), pairs)

        def weight_next(s):
            arrived[s] = line_step(
                arrived[s - 1], range(s - 1, line - 1), range(1, line - s + 1)
            )

        def falls(a, j):
            return a + j < line if a < line // 2 else a < j

        def fell(j):
            table = [int(falls(a, j)) for a in chips]
            flag = jnp.int32(table[-1])
            for a in range(line - 1):
                flag = jnp.where(z == a, table[a], flag)
            return flag

        def holders(j):
            return lambda a: [nh * falls(a, j) + i for i in halves]

        def weight_mine(j):
            block = arrived[j]
            if 2 * j > line:
                straight = jnp.where(lower, z + j < line, z >= j)
                block = jnp.where(straight, block, arrived[line - j])
            mine[j] = block
            pairs = [
                (dev(a, h, g), dev(a, (h + nh) % lo, 1 - g))
                for g in range(2)
                for a in chips
                for h in holders(j)(a)
            ]
            twin[j] = lax.ppermute(block, ("groups", "fsdp"), pairs)

        def spread(j, core):
            held = jnp.where((core >= nh) == (fell(j) == 1), mine[j], twin[j])
            whole[j] = [held] + [to_chip(held, every, o) for o in range(1, lo)]

        numbers, at = [], {}

        def number(name, value):
            at[name] = len(numbers)
            numbers.append(jnp.asarray(value, jnp.int32))

        number("z", z)
        number("half", lax.rem(core, nh) if nh > 1 else 0)
        number("own", core // 2)
        number("odd", lax.rem(core, 2))
        number("other", rising != lower)
        for s in range(1, line):
            number(("hop", s), jnp.where(rising, z > s, z < line - 1 - s))
        for j in range(members):
            number(("to", j), lax.rem(member + members - j, members))
        for k in range(1, line):
            number(("send", k), lax.rem(jnp.where(lower, z - k, z + k) + line, line))
            onward = jnp.where(rising, z + line - k, z - line + k)
            number(("keep", k), jnp.clip(onward, 0, line - 1))
        source = [lax.rem(core + lo - o, lo) for o in range(lo)]
        for j in range(line):
            number(("slot", j), lax.rem(jnp.where(lower, z + j, z - j) + line, line))
            if j == 0:
                places = source
            else:
                down = fell(j)
                first = jnp.where(down == 1, 1 - group, group)
                places = [
                    jnp.where((h // nh) == down, first, 1 - first) * nh + h % nh for h in source
                ]
            for p, value in enumerate(places):
                number(("piece", j, p), value)
        ids = jnp.stack(numbers)

        kept = [None]

        def use_weight(first, n, ids):
            kept[0] = weight_slots(
                ids,
                at[("slot", first)],
                lo,
                [x for j in range(first, first + n) for x in whole[j]],
                width,
                scaled,
                out_grad,
                gate,
                up,
                in_scale,
                slot,
                kept[0],
            )

        weight_first()
        made = prepare(gate, up, in_scale, out_grad, out_scale, slot, line, nh)
        turned, scaled = list(made[:2]), list(made[2:])
        lefts, rights = [turned], [scaled]
        for o in range(1, lo):
            rights.append([to_chip(x, every, o) for x in scaled])
            lefts.append([to_chip(x, every, o) for x in turned])

        got = [None] * line

        def works(a, c, k):
            if k == 0:
                return True
            if a < line // 2:
                return (c < nh) == (k > a)
            return (c >= nh) == (k > line - 1 - a)

        def exchange(k, blocks):
            got[k] = []
            for j in range(1, members):
                pairs = [
                    (dev(a, c, (m + j) % members), dev(a, c, m))
                    for m in range(members)
                    for a in chips
                    for c in range(lo)
                    if works(a, c, k)
                ]
                got[k].append(lax.ppermute(blocks[j - 1], ("member", "fsdp"), pairs))

        others = [at[("to", j)] for j in range(1, members)]
        items = [(at[("send", 1)], j, BF16) for j in range(members - 1)]
        ids, arrived[1] = tie(ids, arrived[1])
        made = partials(ids, at, items, others, lefts, rights, members)
        behind = weight
        exchange(1, made)
        if line > 2:
            weight_next(2)
        weight_mine(1)
        whole[0] = [weight] + [to_chip(behind, every, o) for o in range(1, lo)]
        ids, whole[0] = tie(ids, whole[0])
        order = list(range(2, line)) + [0]
        items = []
        for k in order:
            row = at[("send", k)] if k else None
            items += [(row, j, BF16) for j in range(1, members)]
        for k in order:
            row = at[("keep", k)] if k else None
            items.append((row, 0, BF16 if k else F32))
        items.append((at[("keep", 1)], 0, BF16))
        made = partials(ids, at, items, [at[("to", 0)]] + others, lefts, rights, members)
        twin[1], made = tie(twin[1], made)
        to_send = {
            k: made[n * (members - 1) : (n + 1) * (members - 1)] for n, k in enumerate(order)
        }
        sums = dict(zip(order + [1], made[len(order) * (members - 1) :]))

        coming = []
        joint = shard == weight.shape[0] and columns * 2 == weight.shape[1]

        def line_sum(s):
            return hop(
                ids,
                (at["other"], at[("hop", s)]),
                sums[s],
                list(got[s]),
                list(got[line - s]) if 2 * s > line else [],
                list(coming),
                [arrived[s + 1]] if s + 2 < line and joint else [],
            )

        def line_send(s, total):
            rises, falls = list(range(s)), list(range(line - s, line))
            if s + 2 < line and joint:
                rises += range(s + 1, line - 1)
                falls += range(1, line - 1 - s)
                arrived[s + 2] = line_step(total, rises, falls)
                coming[:] = [arrived[s + 2]]
                return
            coming[:] = [line_step(total, rises, falls)]
            if s + 2 < line:
                weight_next(s + 2)

        spread(1, core)
        whole[1][0], got[1] = tie(whole[1][0], got[1])
        for s in range(1, line):
            k = s + 1 if s + 1 < line else 0
            to_send[k], got[s] = tie(to_send[k], got[s])
            total = line_sum(s)
            ids, total = tie(ids, total)
            here, total = tie(core, total)
            line_send(s, total)
            exchange(k, to_send[k])
            if s + 1 < line:
                weight_mine(s + 1)
            if s > 1:
                spread(s, here)
            first = s if s > 1 else 0
            use_weight(first, s + 1 - first, ids)
            if s + 1 < line:
                (got[k], coming[0]), kept[0] = tie((got[k], coming[0]), kept[0])
                twin[s + 1], kept[0] = tie(twin[s + 1], kept[0])
                if s + 2 < line and joint:
                    arrived[s + 2] = coming[0]
        both = jnp.concatenate(kept[0][2:], axis=1)
        if lo & (lo - 1):
            both = lax.psum(both, "fsdp")
        else:
            stage = 1
            while stage < lo:
                both = both + lax.ppermute(both, "fsdp", [(i, i ^ stage) for i in range(fsdp)])
                stage *= 2
            terms = [both] + [
                lax.ppermute(both, "fsdp", [((i + r * lo) % fsdp, i) for i in range(fsdp)])
                for r in range(1, line)
            ]
            (got[0], coming[0]), terms[1] = tie((got[0], coming[0]), terms[1])
            both = None
            for a in chips:
                term = terms[0]
                for r in range(1, line):
                    term = jnp.where(lax.rem(z + r, line) == a, terms[r], term)
                both = term if both is None else both + term
        top, bottom = coming[0][:, :columns], coming[0][:, columns:]
        landed = []
        for part in range(2):
            pairs = [(i, 2 * i + part) for i in halves]
            pairs += [(nh + i, 2 * i + 1 - part) for i in halves]
            x = jnp.where(rising, bottom, top) if part else jnp.where(rising, top, bottom)
            if any(c != d for c, d in pairs):
                x = lax.ppermute(
                    x, "fsdp", [(dev(a, c), dev(a, d)) for a in chips for c, d in pairs]
                )
            landed.append(x)
        grad_down = sums[0]
        for x in got[0] + landed:
            grad_down = grad_down + x.astype(F32)
        return kept[0][0], kept[0][1], grad_down, both[:, :ff], both[:, ff:]

    return run


def solution(mesh):
    rows = P(("groups", "member", "fsdp"), None)
    in_specs = (
        rows,
        rows,
        rows,
        P("member", None),
        P("member", None),
        P("fsdp", None),
        P(("groups", "member", "fsdp")),
    )
    out_specs = (
        rows,
        rows,
        P(("groups", "fsdp"), "member"),
        P(("groups", "member"), None),
        P(("groups", "member"), None),
    )
    run = on_device(mesh.shape["groups"], mesh.shape["member"], mesh.shape["fsdp"])
    return jax.shard_map(run, mesh=mesh, in_specs=in_specs, out_specs=out_specs, check_vma=False)
```

```python
import functools
import math

import jax
import jax.numpy as jnp
from jax import lax
from jax.experimental import pallas as pl
from jax.experimental.pallas import tpu as pltpu
from jax.sharding import PartitionSpec as P

F32 = jnp.float32
BF16 = jnp.bfloat16
VMEM_BYTES = 60 * 1024 * 1024
ROOT_2_PI = math.sqrt(2.0 / math.pi)
CUBIC = 0.044715
SHORT = pl.CostEstimate(flops=1, bytes_accessed=1, transcendentals=0)


def tanh_of(x):
    return jnp.tanh(ROOT_2_PI * (x + CUBIC * (x * x * x)))


def pick_rows(slot, scale):
    rows = jnp.zeros((slot.shape[0], scale.shape[1]), F32)
    for k in range(scale.shape[0]):
        rows = jnp.where(slot == k, scale[k : k + 1, :], rows)
    return rows


def prepare_kernel(nh, gate_ref, up_ref, in_scale_ref, grad_ref, out_scale_ref, slot_ref, *outs):
    slot = slot_ref[...]
    gate = gate_ref[...].astype(F32)
    gelu = gate * (0.5 * (1.0 + tanh_of(gate)))
    act = gelu * up_ref[...].astype(F32)
    turned = (act * pick_rows(slot, in_scale_ref[...])).T.astype(BF16)
    shard = outs[0].shape[1] // nh
    for i in range(nh):
        for p in range(2):
            first = (2 * i + p) * shard
            outs[p][0, i * shard : (i + 1) * shard, :] = turned[first : first + shard]
    scaled = (grad_ref[...].astype(F32) * pick_rows(slot, out_scale_ref[...])).astype(BF16)
    half = scaled.shape[0] // 2
    outs[2][...] = scaled[:half]
    outs[3][...] = scaled[half:]


def prepare(gate, up, in_scale, out_grad, out_scale, slot, blocks, nh):
    tokens, ff = gate.shape
    d = out_grad.shape[1]
    width, columns = ff // blocks, d // blocks
    mem = in_scale.shape[0]
    spec = lambda shape: pl.BlockSpec(shape, lambda i: (0, i))
    turned = jax.ShapeDtypeStruct((blocks, width // 2, tokens), BF16)
    scaled = jax.ShapeDtypeStruct((tokens // 2, d), BF16)
    return pl.pallas_call(
        functools.partial(prepare_kernel, nh),
        out_shape=[turned, turned, scaled, scaled],
        grid=(blocks,),
        in_specs=[
            spec((tokens, width)),
            spec((tokens, width)),
            spec((mem, width)),
            spec((tokens, columns)),
            spec((mem, columns)),
            pl.BlockSpec((tokens, 1), lambda i: (0, 0)),
        ],
        out_specs=[pl.BlockSpec((1, width // 2, tokens), lambda i: (i, 0, 0))] * 2
        + [spec((tokens // 2, columns))] * 2,
        compiler_params=pltpu.CompilerParams(vmem_limit_bytes=VMEM_BYTES),
        cost_estimate=SHORT,
    )(gate, up, in_scale, out_grad, out_scale, slot)


def partials_kernel(lo, items, n_columns, own_at, ids_ref, *refs):
    lefts, refs = [refs[2 * i : 2 * i + 2] for i in range(lo)], refs[2 * lo :]
    if own_at is not None:
        owns, refs = [refs[2 * i : 2 * i + 2] for i in range(lo)], refs[2 * lo :]
    rights = []
    for _ in range(n_columns):
        rights.append(jnp.concatenate([r[...] for r in refs[: 2 * lo]], axis=0))
        refs = refs[2 * lo :]
    single = lefts[0][0].shape[0] == 1
    for (row, column, _), out in zip(items, refs):
        if row is None:
            odd = ids_ref[own_at] == 1
            left = jnp.concatenate([jnp.where(odd, b[0], a[0]) for a, b in owns], axis=1)
            total = jnp.dot(left, rights[column], preferred_element_type=F32)
            out[...] = total.astype(out.dtype)
            continue
        block = 0 if single else ids_ref[row]
        shard = lefts[0][0].shape[1]
        for p in range(2):
            left = jnp.concatenate([pair[p][block] for pair in lefts], axis=1)
            total = jnp.dot(left, rights[column], preferred_element_type=F32)
            out[p * shard : (p + 1) * shard, :] = total.astype(out.dtype)


def partials(ids, at, items, column_at, lefts, rights, members):
    lo = len(lefts)
    line, part, tokens = lefts[0][0].shape
    shard = part // (lo // 2)
    width = rights[0][0].shape[1] // members
    single = len({row for row, _, _ in items}) == 1
    tile = max(width // 2, 128)
    tiles = width // tile
    if single:
        row = items[0][0]
        left_spec = pl.BlockSpec((1, shard, tokens), lambda i, ids: (ids[row], ids[at["half"]], 0))
    else:
        left_spec = pl.BlockSpec((line, shard, tokens), lambda i, ids: (0, ids[at["half"]], 0))
    flat = [x for pair in lefts for x in pair]
    ins, specs = list(flat), [left_spec] * len(flat)
    own_at = None
    if any(row is None for row, _, _ in items):
        own_at = at["odd"]
        ins += flat
        specs += [
            pl.BlockSpec((1, shard, tokens), lambda i, ids: (ids[at["z"]], ids[at["own"]], 0))
        ] * len(flat)
    for where in column_at:
        ins += [x for pair in rights for x in pair]
        specs += [
            pl.BlockSpec((tokens // 2, tile), lambda i, ids, w=where: (0, ids[w] * tiles + i))
        ] * (2 * lo)
    shapes = [
        jax.ShapeDtypeStruct((shard if row is None else 2 * shard, width), dtype)
        for row, _, dtype in items
    ]
    return pl.pallas_call(
        functools.partial(partials_kernel, lo, items, len(column_at), own_at),
        out_shape=shapes,
        grid_spec=pltpu.PrefetchScalarGridSpec(
            num_scalar_prefetch=1,
            grid=(tiles,),
            in_specs=specs,
            out_specs=[pl.BlockSpec((s.shape[0], tile), lambda i, ids: (0, i)) for s in shapes],
        ),
        compiler_params=pltpu.CompilerParams(vmem_limit_bytes=VMEM_BYTES),
        cost_estimate=SHORT,
    )(ids, *ins)


def hop_kernel(n_got, either, n_coming, flags, ids_ref, sum_ref, *refs):
    gots, refs = refs[: n_got * (1 + either)], refs[n_got * (1 + either) :]
    out_ref = refs[-1]
    total = sum_ref[...].astype(F32)
    for i in range(n_got):
        one = gots[i][...].astype(F32)
        if either:
            one = jnp.where(ids_ref[flags[0]] == 1, gots[n_got + i][...].astype(F32), one)
        total = total + one
    for i in range(n_coming):
        total = total + refs[i][...].astype(F32)
    if len(refs) > n_coming + 1:
        total = jnp.where(ids_ref[flags[1]] == 1, refs[n_coming][...].astype(F32), total)
    out_ref[...] = total.astype(BF16)


def hop(ids, flags, own, got, other, coming, weight):
    rows, columns = own.shape
    stacked = pl.BlockSpec((rows // 2, columns), lambda i, ids: (i, 0))
    beside = pl.BlockSpec((rows // 2, columns), lambda i, ids: (0, i))
    ins = [own] + got + other + coming + weight
    return pl.pallas_call(
        functools.partial(hop_kernel, len(got), bool(other), len(coming), flags),
        out_shape=jax.ShapeDtypeStruct((rows // 2, 2 * columns), BF16),
        grid_spec=pltpu.PrefetchScalarGridSpec(
            num_scalar_prefetch=1,
            grid=(2,),
            in_specs=[stacked] * (1 + len(got) + len(other))
            + [beside] * (len(coming) + len(weight)),
            out_specs=beside,
        ),
        compiler_params=pltpu.CompilerParams(vmem_limit_bytes=VMEM_BYTES),
        cost_estimate=SHORT,
    )(ids, *ins)


def slot_kernel(n, lo, kept, base, ids_ref, *refs):
    pieces, refs = refs[: n * lo], refs[n * lo :]
    scaled_refs, refs = refs[:2], refs[2:]
    out_grad_ref, gate_ref, up_ref, in_scale_ref, slot_ref = refs[:5]
    refs = refs[5:]
    if kept:
        before_ref, refs = refs[3], refs[4:]
    grad_gate_ref, grad_up_ref, sum_in_ref, sum_out_ref, weight_ref, sems = refs
    shard = pieces[0].shape[0]

    step = pl.program_id(0)

    def copy_of(i, p):
        start = pl.multiple_of(ids_ref[base + i * (lo + 1) + 1 + p] * shard, shard)
        return pltpu.make_async_copy(
            pieces[i * lo + p], weight_ref.at[i, pl.ds(start, shard)], sems.at[i, p]
        )

    @pl.when(step == 0)
    def _():
        for i in range(n):
            for p in range(lo):
                copy_of(i, p).start()

    slot = slot_ref[...]
    gate = gate_ref[...].astype(F32)
    up = up_ref[...].astype(F32)
    tanh = tanh_of(gate)
    cdf = 0.5 * (1.0 + tanh)
    slope = cdf + gate * (0.5 * ROOT_2_PI) * (1.0 - tanh * tanh) * (
        1.0 + (3.0 * CUBIC) * (gate * gate)
    )
    gelu = gate * cdf
    act = gelu * up
    row_in = pick_rows(slot, in_scale_ref[...])
    hidden = (act * row_in).astype(BF16)

    for i in range(n):

        @pl.when(step == i)
        def _():
            for p in range(lo):
                copy_of(i, p).wait()

    weight = weight_ref[step]
    scaled = jnp.concatenate([r[...] for r in scaled_refs], axis=0)
    grad_hidden = lax.dot_general(
        scaled, weight, (((1,), (1,)), ((), ())), preferred_element_type=F32
    )
    grad_act = grad_hidden * row_in
    grad_gate_ref[...] = (grad_act * up * slope).astype(BF16)
    grad_up_ref[...] = (grad_act * gelu).astype(BF16)
    product = grad_hidden * act
    forward = jnp.dot(hidden, weight, preferred_element_type=F32)
    forward = forward * out_grad_ref[...].astype(F32)
    mores = []
    for k in range(in_scale_ref.shape[0]):
        mine = slot == k
        row = slice(k, k + 1)
        sum_in_ref[row, :] = jnp.sum(jnp.where(mine, product, 0.0), axis=0, keepdims=True)
        more = jnp.sum(jnp.where(mine, forward, 0.0), axis=0, keepdims=True)
        mores.append(more)

    @pl.when(step == 0)
    def _():
        for k, more in enumerate(mores):
            row = slice(k, k + 1)
            sum_out_ref[row, :] = before_ref[row, :] + more if kept else more

    @pl.when(step > 0)
    def _():
        for k, more in enumerate(mores):
            row = slice(k, k + 1)
            sum_out_ref[row, :] = sum_out_ref[row, :] + more


def weight_slots(ids, base, lo, pieces, width, scaled, out_grad, gate, up, in_scale, slot, kept):
    tokens, ff = gate.shape
    d = out_grad.shape[1]
    mem = in_scale.shape[0]
    n = len(pieces) // lo
    column = lambda rows: pl.BlockSpec(
        (rows, width), lambda i, ids: (0, ids[base + i * (lo + 1)])
    )
    full = lambda shape: pl.BlockSpec(shape, lambda i, ids: (0, 0))
    anywhere = pl.BlockSpec(memory_space=pl.ANY)
    ins = list(pieces) + list(scaled) + [out_grad, gate, up, in_scale, slot]
    specs = [anywhere] * len(pieces) + [full((tokens // 2, d))] * 2
    specs += [full((tokens, d)), column(tokens), column(tokens), column(mem), full((tokens, 1))]
    aliases = {}
    if kept is not None:
        aliases = {1 + len(ins) + i: i for i in range(3)}
        ins += list(kept)
        specs += [anywhere] * 3 + [full((mem, d))]
    return pl.pallas_call(
        functools.partial(slot_kernel, n, lo, kept is not None, base),
        out_shape=[
            jax.ShapeDtypeStruct((tokens, ff), BF16),
            jax.ShapeDtypeStruct((tokens, ff), BF16),
            jax.ShapeDtypeStruct((mem, ff), F32),
            jax.ShapeDtypeStruct((mem, d), F32),
        ],
        grid_spec=pltpu.PrefetchScalarGridSpec(
            num_scalar_prefetch=1,
            grid=(n,),
            in_specs=specs,
            out_specs=[column(tokens), column(tokens), column(mem), full((mem, d))],
            scratch_shapes=[
                pltpu.VMEM((n, width, d), BF16),
                pltpu.SemaphoreType.DMA((n, lo)),
            ],
        ),
        input_output_aliases=aliases,
        compiler_params=pltpu.CompilerParams(vmem_limit_bytes=VMEM_BYTES),
        cost_estimate=SHORT,
    )(ids, *ins)


def on_device(groups, members, fsdp):
    def run(gate, up, out_grad, in_scale, out_scale, weight, member_slot):
        tokens, ff = gate.shape
        shard = weight.shape[0]
        columns = out_grad.shape[1] // members
        lo = max(128 // math.gcd(shard, 128), 2)
        line, nh = fsdp // lo, lo // 2
        assert groups == 2 and line * lo == fsdp and line > 1
        width = lo * shard
        group = lax.axis_index("groups")
        member = lax.axis_index("member")
        place_id = lax.axis_index("fsdp")
        z, core = place_id // lo, lax.rem(place_id, lo)
        lower, rising = z < line // 2, core < nh
        slot = member_slot[:, None]
        chips = range(line)
        halves = range(nh)

        def tie(x, y):
            return lax.optimization_barrier((x, y))

        def dev(zz, c, outer=0):
            return (outer * line + zz) * lo + c

        def line_step(x, rises, falls):
            pairs = [(dev(a, i), dev(a + 1, i)) for a in rises for i in halves]
            pairs += [(dev(a, nh + i), dev(a - 1, nh + i)) for a in falls for i in halves]
            return lax.ppermute(x, "fsdp", pairs)

        def to_chip(x, sources, o):
            return lax.ppermute(
                x, "fsdp", [(dev(a, c), dev(a, (c + o) % lo)) for a in chips for c in sources(a)]
            )

        every = lambda a: range(lo)

        arrived, mine, twin = [None] * line, [None] * line, [None] * line
        whole = [None] * line

        def weight_first():
            pairs = []
            for g in range(2):
                for a in chips:
                    for i in halves:
                        if a + 1 < line:
                            pairs.append((dev(a, g * nh + i, g), dev(a + 1, i, g)))
                        if a > 0:
                            pairs.append((dev(a, (1 - g) * nh + i, g), dev(a - 1, nh + i, g)))
            arrived[1] = lax.ppermute(weight, ("groups", "fsdp"), pairs)

        def weight_next(s):
            arrived[s] = line_step(
                arrived[s - 1], range(s - 1, line - 1), range(1, line - s + 1)
            )

        def falls(a, j):
            return a + j < line if a < line // 2 else a < j

        def fell(j):
            table = [int(falls(a, j)) for a in chips]
            flag = jnp.int32(table[-1])
            for a in range(line - 1):
                flag = jnp.where(z == a, table[a], flag)
            return flag

        def holders(j):
            return lambda a: [nh * falls(a, j) + i for i in halves]

        def weight_mine(j):
            block = arrived[j]
            if 2 * j > line:
                straight = jnp.where(lower, z + j < line, z >= j)
                block = jnp.where(straight, block, arrived[line - j])
            mine[j] = block
            pairs = [
                (dev(a, h, g), dev(a, (h + nh) % lo, 1 - g))
                for g in range(2)
                for a in chips
                for h in holders(j)(a)
            ]
            twin[j] = lax.ppermute(block, ("groups", "fsdp"), pairs)

        def spread(j, core):
            held = jnp.where((core >= nh) == (fell(j) == 1), mine[j], twin[j])
            whole[j] = [held] + [to_chip(held, every, o) for o in range(1, lo)]

        numbers, at = [], {}

        def number(name, value):
            at[name] = len(numbers)
            numbers.append(jnp.asarray(value, jnp.int32))

        number("z", z)
        number("half", lax.rem(core, nh) if nh > 1 else 0)
        number("own", core // 2)
        number("odd", lax.rem(core, 2))
        number("other", rising != lower)
        for s in range(1, line):
            number(("hop", s), jnp.where(rising, z > s, z < line - 1 - s))
        for j in range(members):
            number(("to", j), lax.rem(member + members - j, members))
        for k in range(1, line):
            number(("send", k), lax.rem(jnp.where(lower, z - k, z + k) + line, line))
            onward = jnp.where(rising, z + line - k, z - line + k)
            number(("keep", k), jnp.clip(onward, 0, line - 1))
        source = [lax.rem(core + lo - o, lo) for o in range(lo)]
        for j in range(line):
            number(("slot", j), lax.rem(jnp.where(lower, z + j, z - j) + line, line))
            if j == 0:
                places = source
            else:
                down = fell(j)
                first = jnp.where(down == 1, 1 - group, group)
                places = [
                    jnp.where((h // nh) == down, first, 1 - first) * nh + h % nh for h in source
                ]
            for p, value in enumerate(places):
                number(("piece", j, p), value)
        ids = jnp.stack(numbers)

        kept = [None]

        def use_weight(first, n, ids):
            kept[0] = weight_slots(
                ids,
                at[("slot", first)],
                lo,
                [x for j in range(first, first + n) for x in whole[j]],
                width,
                scaled,
                out_grad,
                gate,
                up,
                in_scale,
                slot,
                kept[0],
            )

        weight_first()
        made = prepare(gate, up, in_scale, out_grad, out_scale, slot, line, nh)
        turned, scaled = list(made[:2]), list(made[2:])
        lefts, rights = [turned], [scaled]
        for o in range(1, lo):
            rights.append([to_chip(x, every, o) for x in scaled])
            lefts.append([to_chip(x, every, o) for x in turned])

        got = [None] * line

        def works(a, c, k):
            if k == 0:
                return True
            if a < line // 2:
                return (c < nh) == (k > a)
            return (c >= nh) == (k > line - 1 - a)

        def exchange(k, blocks):
            got[k] = []
            for j in range(1, members):
                pairs = [
                    (dev(a, c, (m + j) % members), dev(a, c, m))
                    for m in range(members)
                    for a in chips
                    for c in range(lo)
                    if works(a, c, k)
                ]
                got[k].append(lax.ppermute(blocks[j - 1], ("member", "fsdp"), pairs))

        others = [at[("to", j)] for j in range(1, members)]
        items = [(at[("send", 1)], j, BF16) for j in range(members - 1)]
        ids, arrived[1] = tie(ids, arrived[1])
        made = partials(ids, at, items, others, lefts, rights, members)
        behind = weight
        exchange(1, made)
        if line > 2:
            weight_next(2)
        weight_mine(1)
        whole[0] = [weight] + [to_chip(behind, every, o) for o in range(1, lo)]
        ids, whole[0] = tie(ids, whole[0])
        order = list(range(2, line)) + [0]
        items = []
        for k in order:
            row = at[("send", k)] if k else None
            items += [(row, j, BF16) for j in range(1, members)]
        for k in order:
            row = at[("keep", k)] if k else None
            items.append((row, 0, BF16 if k else F32))
        items.append((at[("keep", 1)], 0, BF16))
        made = partials(ids, at, items, [at[("to", 0)]] + others, lefts, rights, members)
        twin[1], made = tie(twin[1], made)
        to_send = {
            k: made[n * (members - 1) : (n + 1) * (members - 1)] for n, k in enumerate(order)
        }
        sums = dict(zip(order + [1], made[len(order) * (members - 1) :]))

        coming = []
        joint = shard == weight.shape[0] and columns * 2 == weight.shape[1]

        def line_sum(s):
            return hop(
                ids,
                (at["other"], at[("hop", s)]),
                sums[s],
                list(got[s]),
                list(got[line - s]) if 2 * s > line else [],
                list(coming),
                [arrived[s + 1]] if s + 2 < line and joint else [],
            )

        def line_send(s, total):
            rises, falls = list(range(s)), list(range(line - s, line))
            if s + 2 < line and joint:
                rises += range(s + 1, line - 1)
                falls += range(1, line - 1 - s)
                arrived[s + 2] = line_step(total, rises, falls)
                coming[:] = [arrived[s + 2]]
                return
            coming[:] = [line_step(total, rises, falls)]
            if s + 2 < line:
                weight_next(s + 2)

        spread(1, core)
        whole[1][0], got[1] = tie(whole[1][0], got[1])
        for s in range(1, line):
            k = s + 1 if s + 1 < line else 0
            to_send[k], got[s] = tie(to_send[k], got[s])
            total = line_sum(s)
            ids, total = tie(ids, total)
            here, total = tie(core, total)
            line_send(s, total)
            exchange(k, to_send[k])
            if s + 1 < line:
                weight_mine(s + 1)
            if s > 1:
                spread(s, here)
            first = s if s > 1 else 0
            use_weight(first, s + 1 - first, ids)
            if s + 1 < line:
                (got[k], coming[0]), kept[0] = tie((got[k], coming[0]), kept[0])
                twin[s + 1], kept[0] = tie(twin[s + 1], kept[0])
                if s + 2 < line and joint:
                    arrived[s + 2] = coming[0]
        both = jnp.concatenate(kept[0][2:], axis=1)
        if lo & (lo - 1):
            both = lax.psum(both, "fsdp")
        else:
            stage = 1
            while stage < lo:
                both = both + lax.ppermute(both, "fsdp", [(i, i ^ stage) for i in range(fsdp)])
                stage *= 2
            terms = [both] + [
                lax.ppermute(both, "fsdp", [((i + r * lo) % fsdp, i) for i in range(fsdp)])
                for r in range(1, line)
            ]
            (got[0], coming[0]), terms[1] = tie((got[0], coming[0]), terms[1])
            both = None
            for a in chips:
                term = terms[0]
                for r in range(1, line):
                    term = jnp.where(lax.rem(z + r, line) == a, terms[r], term)
                both = term if both is None else both + term
        top, bottom = coming[0][:, :columns], coming[0][:, columns:]
        landed = []
        for part in range(2):
            pairs = [(i, 2 * i + part) for i in halves]
            pairs += [(nh + i, 2 * i + 1 - part) for i in halves]
            x = jnp.where(rising, bottom, top) if part else jnp.where(rising, top, bottom)
            if any(c != d for c, d in pairs):
                x = lax.ppermute(
                    x, "fsdp", [(dev(a, c), dev(a, d)) for a in chips for c, d in pairs]
                )
            landed.append(x)
        grad_down = sums[0]
        for x in got[0] + landed:
            grad_down = grad_down + x.astype(F32)
        return kept[0][0], kept[0][1], grad_down, both[:, :ff], both[:, ff:]

    return run


def solution(mesh):
    rows = P(("groups", "member", "fsdp"), None)
    in_specs = (
        rows,
        rows,
        rows,
        P("member", None),
        P("member", None),
        P("fsdp", None),
        P(("groups", "member", "fsdp")),
    )
    out_specs = (
        rows,
        rows,
        P(("groups", "fsdp"), "member"),
        P(("groups", "member"), None),
        P(("groups", "member"), None),
    )
    run = on_device(mesh.shape["groups"], mesh.shape["member"], mesh.shape["fsdp"])
    return jax.shard_map(run, mesh=mesh, in_specs=in_specs, out_specs=out_specs, check_vma=False)
```
